32 devices in a mesh: runs: 2 (over y), sec: 4 (over z), mpo: 2 (over x), rep: 2 (over core).
Axes of the slice: x: 2, y: 2, z: 4, core: 2. Of those that a mesh axis runs over, the one named last changes fastest.
Arguments:
- psi: bfloat16 [32, 128, 16, 128], P(('runs', 'sec', 'rep')), parts along dimension 0, may hold values from -6 to 6
- dims: int32 [32], P('runs'), parts along dimension 0, may hold values from 1 to 128, 1280 in all
- left_env: bfloat16 [16, 32, 128, 128], P('mpo', ('runs', 'sec', 'rep')), parts along dimension 1, may hold values from -0.5 to 0.5
- right_env: bfloat16 [16, 32, 128, 128], P('mpo', ('runs', 'sec', 'rep')), parts along dimension 1, may hold values from -0.5 to 0.5
- shift: int32 [16], P('mpo'), may hold values from -2 to 2, as said below
- mpo_coef: bfloat16 [16, 16, 16, 16], P('mpo'), may hold values from -0.09375 to 0.09375
- mpo_mask: int32 [16, 16], P('mpo'), may hold values 0 or 1
Outputs:
- result: bfloat16 [32, 128, 16, 128], P(('runs', 'sec', 'rep'), None, 'mpo'), parts along dimension 0
The draws below stay inside these ranges and needn't reach their ends.
There are 2 independent parts, one for each index of `runs`. The reference program is written for one: setup_inputs(seed, part) draws one part's arguments, and reference() takes and returns one part's arrays. A program takes and returns all parts, laid end to end along the dimension named above; an argument that names none is the same for every part. Nothing has to cross between parts.
Inputs may be any that keep to these rules, and one draw needn't show every extreme that they name: `shift`: every offset from -2 to 2 is carried by some channel.
All inputs are finite; a program needn't handle non-finite values. No bound on the sum of `mpo_mask` on one device may be relied on, other than what follows from the above.
Results may differ from the reference program's by a relative error of at most 0.011.
Values may be sent and summed in bfloat16 or wider, within the bound.
No kernel may reach another device: no remote copies, remote signals or barrier semaphores. Data moves between devices by JAX's collectives and lax.ppermute only.
A program may use at most 128 MiB of HBM per device.

```python
import math
import jax
import jax.numpy as jnp
import numpy as np
from jax import lax

BD = 128
PH = 16
W_DEV = 8
SEC_DEV = 2
GROUPS = 2
W = 16
SECTORS = 16


def draw_shift(key, part):
    key = jax.random.fold_in(key, 7)
    base = (jnp.arange(W, dtype=jnp.int32) % (2 * SEC_DEV + 1) - SEC_DEV).astype(jnp.int32)
    return jax.random.permutation(key, base)


def with_ends(array, stream_key, low, top_value):
    longest = array.shape.index(max(array.shape))
    spots = []
    for shift in (0, 1):
        where = [jax.random.randint(jax.random.fold_in(stream_key, axis), (), 0, length) for axis, length in enumerate(array.shape)]
        where[longest] = (where[longest] + shift) % array.shape[longest]
        spots.append(tuple(where))
    return array.at[spots[0]].set(low).at[spots[1]].set(top_value)


def block_scale(key, shape, pieces, low, high):
    gain = 1.0
    for dim, shards_of in pieces:
        heights = jax.random.uniform(jax.random.fold_in(jax.random.fold_in(key, 6), dim), (shards_of,), jnp.float32, low / len(pieces), high / len(pieces))
        gain = gain * jnp.repeat(jnp.exp(heights), shape[dim] // shards_of).reshape((-1,) + (1,) * (len(shape) - 1 - dim))
    return gain


def split_up(count, total, reach, skew):
    portions = [(1 << 20) // math.isqrt(standing ** skew) + 1 for standing in range(2, count + 1)]
    rest, given = total - reach - (count - 1), [1] * (count - 1)
    while rest > 0:
        movable = [i for i in range(count - 1) if given[i] < reach]
        pool, budget = sum([portions[i] for i in movable]), rest
        for i in movable:
            addition = min(reach - given[i], max(1, budget * portions[i] // pool), rest)
            given[i] = given[i] + addition
            rest = rest - addition
    return np.array([reach] + given)


def uneven_parts(key, number_of, total, reach, skew):
    if number_of == 2:
        one = jax.random.randint(key, (), max(1, total - reach), min(reach, total - 1) + 1)
        return jnp.stack([one, total - one])
    sizes = jnp.asarray(split_up(number_of, total, reach, skew), jnp.int32)
    pairs = (number_of - 1) // 2
    source_of, sink = sizes[1:1 + 2 * pairs:2], sizes[2:2 + 2 * pairs:2]
    margin = jnp.minimum(source_of - 1, reach - sink)
    shifted = jax.random.randint(jax.random.fold_in(key, 1), (pairs,), 0, 1 << 20) % (margin + 1)
    sizes = sizes.at[1:1 + 2 * pairs:2].set(source_of - shifted).at[2:2 + 2 * pairs:2].set(sink + shifted)
    return sizes[jax.random.permutation(jax.random.fold_in(key, 2), number_of)]


def scatter_about(stream_key, shape, spread, limit, cuts=(), kind=jnp.bfloat16):
    entries = jax.random.normal(stream_key, shape, jnp.float32) * spread
    if len(cuts) > 0:
        entries = block_scale(stream_key, shape, cuts, -0.22, 0.18) * entries
    return jnp.clip(entries, min=-limit, max=limit).astype(kind)


def setup_inputs(seed: int = 0, part: int = 0) -> dict:
    seeds = jax.random.split(jax.random.key(seed), 8)
    part_splits = jax.random.split(jax.random.fold_in(seeds[7], part), 8)
    return {
        "psi": scatter_about(part_splits[0], (SECTORS, BD, PH, BD), 1.0, 6.0, ((0, 8),)),
        "dims": uneven_parts(part_splits[1], SECTORS, SECTORS * BD * 5 // 8, BD, 1).astype(jnp.int32),
        "left_env": scatter_about(part_splits[2], (W, SECTORS, BD, BD), BD ** -0.5, 0.5, ((0, 2), (1, 8))),
        "right_env": scatter_about(part_splits[3], (W, SECTORS, BD, BD), BD ** -0.5, 0.5, ((0, 2), (1, 8))),
        "shift": draw_shift(jax.random.fold_in(seeds[7], 71), part),
        "mpo_coef": scatter_about(seeds[5], (W, W, PH, PH), (W * W * PH) ** -0.5, 0.09375, ((0, 2),)),
        "mpo_mask": with_ends((jax.random.randint(seeds[6], (W, W), 0, 2) < 1).astype(jnp.int32), jax.random.fold_in(seeds[6], 1), 0, 1),
    }


def reference(psi, dims, left_env, right_env, shift, mpo_coef, mpo_mask):
    total = psi.shape[0]
    block = psi.shape[1]
    lanes = jnp.arange(block, dtype=jnp.int32)
    row_keep = lanes[None, :] < dims[:, None]
    col_keep = lanes[None, :] < dims[::-1][:, None]
    keep = row_keep[:, :, None, None] & col_keep[:, None, None, :]
    masked = psi * keep.astype(jnp.bfloat16)
    border = jnp.zeros((SEC_DEV,) + psi.shape[1:], jnp.bfloat16)
    extended = jnp.concatenate([border, masked, border], axis=0)
    coupling = mpo_coef * mpo_mask.astype(jnp.bfloat16)[:, :, None, None]
    grouped_coupling = coupling.astype(jnp.float32).reshape(GROUPS, W_DEV, W, PH, PH)
    right_mirror = right_env[:, ::-1]

    def one_sector(sector):
        places = (sector + SEC_DEV - shift).astype(jnp.int32)
        sources = jnp.take(extended, places, axis=0)
        left_k = lax.dynamic_index_in_dim(left_env, sector, 1, keepdims=False)
        first = jnp.einsum('wac,wcsb->wasb', left_k.astype(jnp.float32), sources.astype(jnp.float32)).astype(jnp.bfloat16)
        grouped = first.astype(jnp.float32).reshape(GROUPS, W_DEV, block, PH, block)
        mixed = jnp.einsum('gwvst,gwatb->gvasb', grouped_coupling, grouped).astype(jnp.bfloat16)
        right_k = lax.dynamic_index_in_dim(right_mirror, sector, 1, keepdims=False)
        return jnp.einsum('gvasc,vbc->asb', mixed.astype(jnp.float32), right_k.astype(jnp.float32))

    applied = lax.map(one_sector, jnp.arange(total, dtype=jnp.int32))
    return (applied * keep.astype(jnp.float32)).astype(jnp.bfloat16)
```

```python
import functools

import jax
import jax.numpy as jnp
from jax import lax
from jax.experimental import pallas as pl
from jax.experimental.pallas import tpu as pltpu
from jax.sharding import PartitionSpec as P

F32 = jnp.float32
BF16 = jnp.bfloat16
VMEM = pltpu.VMEM
SMEM = pltpu.SMEM
PAD = 1


def ring(block, axis, step):
    count = lax.axis_size(axis)
    return lax.ppermute(block, axis, [((i + step) % count, i) for i in range(count)])


def mix_kernel(entry, info, dims, shift, own, near, far, left_own, *rest):
    *left_other, coupling, mixed, turned, first, plane = rest
    lefts = [left_own, *left_other]
    _, block, states, width = own.shape
    w_dev = left_own.shape[0]
    place = info[0]
    places = info[1]
    first_sector = place * 2
    sector = first_sector + entry
    rows = lax.broadcasted_iota(jnp.int32, (block, width), 0)
    lanes = lax.broadcasted_iota(jnp.int32, (block, width), 1)
    near_place = place + 1 - 2 * lax.rem(place, 2)
    far_place = place - 1 + 2 * lax.rem(place, 2)
    for which, (ref, home) in enumerate(((own, place), (near, near_place), (far, far_place))):
        for e in range(2):
            source = jnp.clip(home * 2 + e, 0, 2 * places - 1)
            keep = (rows < dims[source]) & (lanes < dims[2 * places - 1 - source])
            plane[...] = ref[e].astype(F32).reshape(block * states, width)
            for t in range(states):
                piece = plane[pl.ds(t, block, stride=states), :]
                turned[which * 2 + e, :, t * width : (t + 1) * width] = jnp.where(
                    keep, piece, 0.0
                ).astype(BF16)
    step = block + PAD

    for j, left in enumerate(lefts):

        def stage1(w, carry, j=j, left=left):
            source = sector - shift[j * w_dev + w]
            at = source >> 1
            which = jnp.where(at == place, 0, jnp.where(at == near_place, 1, 2))
            slot = which * 2 + (source & 1)
            matrix = left[w, entry]
            for t in range(0, states, 2):
                product = jnp.dot(
                    matrix,
                    turned[slot, :, t * width : (t + 2) * width],
                    preferred_element_type=F32,
                )
                for h in range(2):
                    row = ((j * w_dev + w) * states + t + h) * step
                    first[pl.ds(row, block), :] = product[:, h * width : (h + 1) * width]
            return carry

        lax.fori_loop(0, w_dev, stage1, 0)

    inner = len(lefts) * w_dev * states
    outer = coupling.shape[0]
    channels = outer // 8

    def stage2(i, carry):
        for u in range(4):
            a = i * 8 + u * 2
            pair = [first[pl.ds(a + h, inner, stride=step), :].astype(BF16) for h in range(2)]
            product = jnp.dot(
                coupling[...], jnp.concatenate(pair, axis=1), preferred_element_type=F32
            )
            halves = [
                product[:, h * width : (h + 1) * width].reshape(channels, 1, 8, width)
                for h in range(2)
            ]
            both = jnp.concatenate(halves, axis=1).reshape(channels, 16, width).astype(BF16)
            for v in range(channels):
                mixed[pl.ds(pl.multiple_of(a * 8, 16), 16), v * width : (v + 1) * width] = both[v]
        return carry

    lax.fori_loop(0, block // 8, stage2, 0)


def mix(entry, info, dims, shift, psis, lefts, coupling):
    _, block, states, width = psis[0].shape
    channels = coupling.shape[0] // 8
    inner = coupling.shape[1]
    return pl.pallas_call(
        functools.partial(mix_kernel, entry),
        out_shape=jax.ShapeDtypeStruct((block * 8, channels * width), BF16),
        in_specs=[pl.BlockSpec(memory_space=SMEM)] * 3
        + [pl.BlockSpec(memory_space=VMEM)] * (len(psis) + len(lefts) + 1),
        out_specs=pl.BlockSpec(memory_space=VMEM),
        scratch_shapes=[
            VMEM((6, block, states * width), BF16),
            VMEM((inner * (block + PAD), width), F32),
            VMEM((block * states, width), F32),
        ],
        compiler_params=pltpu.CompilerParams(vmem_limit_bytes=(36 if inner <= 256 else 60) << 20),
        cost_estimate=pl.CostEstimate(
            flops=2 * inner * block * width * (block + channels * 8),
            bytes_accessed=8 << 20,
            transcendentals=0,
        ),
        name=f"mix_{entry}",
    )(info, dims, shift, *psis, *lefts, coupling)


def apply_kernel(entry, info, dims, mixed, *rest):
    n = mixed.shape[1] // (rest[0].shape[0] * rest[0].shape[2])
    rights = rest[:n]
    out = rest[-1]
    v_dev, width, depth = rights[0].shape
    block = out.shape[1]
    place, places, group = info[0], info[1], info[2]
    total = jnp.zeros((block * 8, width), F32)
    for j, right in enumerate(rights):
        where = lax.rem(group + j, len(rights)) * v_dev
        for v in range(0, v_dev, 2):
            column = pl.multiple_of((where + v) * depth, 2 * depth)
            weights = jnp.concatenate([right[v], right[v + 1]], axis=1)
            total += lax.dot_general(
                mixed[:, pl.ds(column, 2 * depth)],
                weights,
                (((1,), (1,)), ((), ())),
                preferred_element_type=F32,
            )
    sector = place * 2 + entry
    cube = (block, 8, width)
    keep = (lax.broadcasted_iota(jnp.int32, cube, 0) < dims[sector]) & (
        lax.broadcasted_iota(jnp.int32, cube, 2) < dims[2 * places - 1 - sector]
    )
    out[0] = jnp.where(keep, total.reshape(cube), 0.0).astype(BF16)


def apply(entry, info, dims, mixed, rights, before, width):
    block = mixed.shape[0] // 8
    out_shape = jax.ShapeDtypeStruct((2, block, 8, width), BF16)
    whole = lambda a: pl.BlockSpec(a.shape, lambda i, n=a.ndim: (0,) * n)
    return pl.pallas_call(
        functools.partial(apply_kernel, entry),
        grid=(1,),
        out_shape=out_shape,
        in_specs=[pl.BlockSpec(memory_space=SMEM)] * 2
        + [whole(mixed)]
        + [whole(r) for r in rights]
        + [pl.BlockSpec(memory_space=pl.ANY)] * len(before),
        out_specs=pl.BlockSpec((1, block, 8, width), lambda i: (entry, 0, 0, 0)),
        input_output_aliases={3 + len(rights): 0} if before else {},
        compiler_params=pltpu.CompilerParams(vmem_limit_bytes=32 << 20),
        cost_estimate=pl.CostEstimate(
            flops=2 * mixed.size * width, bytes_accessed=6 << 20, transcendentals=0
        ),
        name=f"apply_{entry}",
    )(info, dims, mixed, *rights, *before)


def on_device(psi, dims, left_env, right_env, shift, mpo_coef, mpo_mask):
    sec_dev, block, states, width = psi.shape
    w_dev = left_env.shape[0]
    groups = lax.axis_size("mpo")
    spots = ("sec", "rep")
    places = lax.axis_size(spots)
    place = lax.axis_index(spots)
    group = lax.axis_index("mpo")
    info = jnp.stack([place, jnp.int32(places), group]).astype(jnp.int32)
    share = states // groups

    def swap(block, begin):
        route = []
        for low in range(begin, places - 1, 2):
            route += [(low, low + 1), (low + 1, low)]
        return lax.ppermute(block, spots, route)

    far = swap(psi, 1)
    near = swap(psi, 0)
    lefts = [left_env] + [ring(left_env, "mpo", j) for j in range(1, groups)]
    mirror = [(i, places - 1 - i) for i in range(places)]
    coupling = mpo_coef * mpo_mask.astype(BF16)[:, :, None, None]
    channels = coupling.shape[1]
    packed = jnp.transpose(coupling, (1, 2, 0, 3)).reshape(channels, states, w_dev * states)
    offsets = jnp.broadcast_to(
        jnp.pad(shift, (0, w_dev * states - w_dev)).astype(BF16), (1, states, w_dev * states)
    )
    packed = jnp.concatenate([packed, offsets], axis=0)
    parcels = [packed] + [ring(packed, "mpo", j) for j in range(1, groups)]
    shifts = jnp.concatenate([p[channels, 0, :w_dev] for p in parcels]).astype(jnp.int32)
    begin = (group * share) // 8 * 8
    matrix = jnp.concatenate(
        [lax.dynamic_slice_in_dim(p[:channels], begin, 8, 1) for p in parcels], axis=2
    ).reshape(channels * 8, groups * w_dev * states)
    psis = [psi, near, far]
    result = ()
    for entry in range(sec_dev):
        chunk = lax.ppermute(right_env[:, sec_dev - 1 - entry], spots, mirror)
        rights = [chunk] + [ring(chunk, "mpo", j) for j in range(1, groups)]
        mixed = mix(entry, info, dims, shifts, psis, lefts, matrix)
        result = (apply(entry, info, dims, mixed, rights, result, width),)
    result = result[0]
    if share != 8:
        result = lax.dynamic_slice_in_dim(result, group * share - begin, share, 2)
    return result


def solution(mesh):
    return jax.shard_map(
        on_device,
        mesh=mesh,
        in_specs=(
            P(("runs", "sec", "rep"), None, None, None),
            P("runs"),
            P("mpo", ("runs", "sec", "rep"), None, None),
            P("mpo", ("runs", "sec", "rep"), None, None),
            P("mpo"),
            P("mpo", None, None, None),
            P("mpo", None),
        ),
        out_specs=P(("runs", "sec", "rep"), None, "mpo", None),
        check_vma=False,
    )
```

```python
import functools

import jax
import jax.numpy as jnp
from jax import lax
from jax.experimental import pallas as pl
from jax.experimental.pallas import tpu as pltpu
from jax.sharding import PartitionSpec as P

F32 = jnp.float32
BF16 = jnp.bfloat16
VMEM = pltpu.VMEM
SMEM = pltpu.SMEM
SMALL = pl.CostEstimate(flops=1 << 10, bytes_accessed=1 << 10, transcendentals=0)
SOME = pl.CostEstimate(flops=1 << 28, bytes_accessed=1 << 20, transcendentals=0)
PAD = 1


def ring(block, axis, step):
    count = lax.axis_size(axis)
    return lax.ppermute(block, axis, [((i + step) % count, i) for i in range(count)])


def turn_kernel(which, info, dims, *refs):
    turned, plane = refs[-2:]
    _, block, states, width = refs[0].shape
    place, places = info[0], info[1]
    odd = lax.rem(place, 2)
    home = (place, place + 1 - 2 * odd, place - 1 + 2 * odd)[which]
    rows = lax.broadcasted_iota(jnp.int32, (block, width), 0)
    lanes = lax.broadcasted_iota(jnp.int32, (block, width), 1)

    def move(psi, entry):
        source = jnp.clip(home * 2 + entry, 0, 2 * places - 1)
        keep = (rows < dims[source]) & (lanes < dims[2 * places - 1 - source])
        plane[...] = psi.astype(F32).reshape(block * states, width)
        for t in range(states):
            piece = plane[pl.ds(t, block, stride=states), :]
            turned[entry, :, t * width : (t + 1) * width] = jnp.where(keep, piece, 0.0).astype(BF16)

    for e in range(2):
        move(refs[0][e], e)


def turn(which, info, dims, psi, *before):
    _, block, states, width = psi.shape
    return pl.pallas_call(
        functools.partial(turn_kernel, which),
        grid=(1,),
        out_shape=jax.ShapeDtypeStruct((6, block, states * width), BF16),
        in_specs=[pl.BlockSpec(memory_space=SMEM)] * 2
        + [pl.BlockSpec(psi.shape, lambda i: (0, 0, 0, 0))]
        + [pl.BlockSpec(memory_space=pl.ANY)] * len(before),
        out_specs=pl.BlockSpec((2, block, states * width), lambda i: (which, 0, 0)),
        scratch_shapes=[VMEM((block * states, width), F32)],
        input_output_aliases={3: 0} if before else {},
        compiler_params=pltpu.CompilerParams(vmem_limit_bytes=16 << 20),
        cost_estimate=SMALL,
        name=f"turn_{which}",
    )(info, dims, psi, *before)


def pack_kernel(info, mask, shift, coef, left, *outs):
    w_dev, channels, states, _ = coef.shape
    block = left.shape[2]
    base = w_dev * block
    lanes = lax.broadcasted_iota(jnp.int32, (states, w_dev * states), 1)
    offsets = jnp.zeros(lanes.shape, F32)
    for w in range(w_dev):
        offsets = jnp.where(lanes == w, shift[w].astype(F32), offsets)
    for j, out in enumerate(outs):
        entry = lax.rem(info[3] + j + 1, 2)
        for w in range(w_dev):
            out[w * block : (w + 1) * block] = left[w, entry]
        for v in range(channels):
            pieces = [coef[w, v].astype(F32) * mask[w, v].astype(F32) for w in range(w_dev)]
            out[base + v * states : base + (v + 1) * states] = jnp.concatenate(
                pieces, axis=1
            ).astype(BF16)
        out[base + channels * states : base + (channels + 1) * states] = offsets.astype(BF16)


def pack(info, mask, shift, coef, left, copies):
    w_dev, channels, states, _ = coef.shape
    rows = w_dev * left.shape[2] + (channels + 1) * states
    return pl.pallas_call(
        pack_kernel,
        out_shape=[jax.ShapeDtypeStruct((rows, w_dev * states), BF16)] * copies,
        in_specs=[pl.BlockSpec(memory_space=SMEM)] * 3 + [pl.BlockSpec(memory_space=VMEM)] * 2,
        out_specs=[pl.BlockSpec(memory_space=VMEM)] * copies,
        compiler_params=pltpu.CompilerParams(vmem_limit_bytes=16 << 20),
        cost_estimate=SMALL,
        name="pack",
    )(info, mask, shift, coef, left)


def cut_env_kernel(entries, rows, info, env, *outs):
    for entry, (begin, size), out in zip(entries, rows, outs):
        at = lax.rem(info[3] + entry, 2)
        for v in range(env.shape[0]):
            out[v] = env[v, at, begin : begin + size, :]


def cut_env(info, env, entries, rows):
    return pl.pallas_call(
        functools.partial(cut_env_kernel, entries, rows),
        out_shape=[
            jax.ShapeDtypeStruct((env.shape[0], size, env.shape[3]), BF16) for _, size in rows
        ],
        in_specs=[pl.BlockSpec(memory_space=SMEM), pl.BlockSpec(memory_space=VMEM)],
        out_specs=[pl.BlockSpec(memory_space=VMEM)] * len(rows),
        compiler_params=pltpu.CompilerParams(vmem_limit_bytes=8 << 20),
        cost_estimate=SMALL,
        name="cut_env",
    )(info, env)


def mix_kernel(info, shift, *refs):
    turned, own, *parcels = refs[:-4]
    given, kept, first, coupling = refs[-4:]
    groups = len(parcels)
    w_dev, _, block, _ = own.shape
    width = block
    states = turned.shape[2] // width
    channels = coupling.shape[0] // 16
    base = w_dev * block
    place, parity = info[0], info[3]
    near_place = place + 1 - 2 * lax.rem(place, 2)
    sector = place * 2 + parity
    step = block + PAD
    for j, parcel in enumerate(parcels):
        cube = parcel[base : base + channels * states].astype(F32)
        cube = cube.reshape(channels, states, w_dev * states)
        for h in range(2):
            rows = jnp.where(info[4 + h] == 0, cube[:, :8], cube[:, 8:]).reshape(channels * 8, -1)
            coupling[
                h * channels * 8 : (h + 1) * channels * 8,
                j * w_dev * states : (j + 1) * w_dev * states,
            ] = rows.astype(BF16)

    for j, parcel in enumerate(parcels):
        for w in range(w_dev):
            source = sector - shift[j * w_dev + w]
            at = source >> 1
            which = jnp.where(at == place, 0, jnp.where(at == near_place, 1, 2))
            slot = which * 2 + (source & 1)
            matrix = own[w, parity] if j == 0 else parcel[w * block : (w + 1) * block]
            for t in range(0, states, 2):
                product = jnp.dot(
                    matrix,
                    turned[slot, :, t * width : (t + 2) * width],
                    preferred_element_type=F32,
                )
                for h in range(2):
                    row = ((j * w_dev + w) * states + t + h) * step
                    first[pl.ds(row, block), :] = product[:, h * width : (h + 1) * width]

    inner = groups * w_dev * states

    def stage2(i, carry):
        for u in range(4):
            a = i * 8 + u * 2
            pair = [first[pl.ds(a + h, inner, stride=step), :].astype(BF16) for h in range(2)]
            product = jnp.dot(
                coupling[...], jnp.concatenate(pair, axis=1), preferred_element_type=F32
            )
            for half, mixed in enumerate((given, kept)):
                part = product[half * channels * 8 : (half + 1) * channels * 8]
                halves = [
                    part[:, h * width : (h + 1) * width].reshape(channels, 1, 8, width)
                    for h in range(2)
                ]
                both = jnp.concatenate(halves, axis=1).reshape(channels, 16, width).astype(BF16)
                for v in range(channels):
                    mixed[pl.ds(pl.multiple_of(a * 8, 16), 16), v * width : (v + 1) * width] = both[
                        v
                    ]
        return carry

    lax.fori_loop(0, block // 8, stage2, 0, unroll=True)


def mix(info, shift, channels, turned, own, parcels):
    _, block, flat = turned.shape
    width = block
    inner = parcels[0].shape[1] * len(parcels)
    return pl.pallas_call(
        mix_kernel,
        out_shape=[jax.ShapeDtypeStruct((block * 8, channels * width), BF16)] * 2,
        in_specs=[pl.BlockSpec(memory_space=SMEM)] * 2
        + [pl.BlockSpec(memory_space=VMEM)] * (2 + len(parcels)),
        out_specs=[pl.BlockSpec(memory_space=VMEM)] * 2,
        scratch_shapes=[
            VMEM((inner * (block + PAD), width), F32),
            VMEM((channels * 16, inner), BF16),
        ],
        compiler_params=pltpu.CompilerParams(vmem_limit_bytes=(40 if inner <= 256 else 62) << 20),
        cost_estimate=SMALL,
        name="mix",
    )(info, shift, turned, own, *parcels)


def product(mixed, rights, wheres):
    total = None
    for right, where in zip(rights, wheres):
        depth = right[0].shape[1]
        column = pl.multiple_of(where * depth, depth)
        part = lax.dot_general(
            mixed[:, pl.ds(column, len(right) * depth)],
            jnp.concatenate(right, axis=1),
            (((1,), (1,)), ((), ())),
            preferred_element_type=F32,
        )
        total = part if total is None else total + part
    return total


def masked(total, info, dims, begin):
    rows, size = total.shape
    sector = info[0] * 2 + info[3]
    cube = (rows // 8, 8, size)
    a = lax.broadcasted_iota(jnp.int32, cube, 0)
    b = lax.broadcasted_iota(jnp.int32, cube, 2) + begin
    keep = (a < dims[sector]) & (b < dims[2 * info[1] - 1 - sector])
    return jnp.where(keep, total.reshape(cube), 0.0)


def begin_kernel(info, given, kept, right, given_out, kept_out):
    v_dev = right.shape[0]
    blocks = [[right[v] for v in range(v_dev)]]
    given_out[...] = product(given, blocks, [info[2] * v_dev])
    kept_out[...] = product(kept, blocks, [info[2] * v_dev])


def begin(info, given, kept, right):
    rows, width = given.shape[0], right.shape[1]
    return pl.pallas_call(
        begin_kernel,
        out_shape=[jax.ShapeDtypeStruct((rows, width), F32)] * 2,
        in_specs=[pl.BlockSpec(memory_space=SMEM)] + [pl.BlockSpec(memory_space=VMEM)] * 3,
        out_specs=[pl.BlockSpec(memory_space=VMEM)] * 2,
        compiler_params=pltpu.CompilerParams(vmem_limit_bytes=24 << 20),
        cost_estimate=SOME,
        name="begin",
    )(info, given, kept, right)


def others(info, v_dev, groups):
    return [lax.rem(info[2] + j, groups) * v_dev for j in range(1, groups)]


def give_kernel(piece, info, dims, mixed, before, *refs):
    rights, out = refs[:-1], refs[-1]
    v_dev, size, _ = rights[0].shape
    blocks = [[right[v] for v in range(v_dev)] for right in rights]
    total = product(mixed, blocks, others(info, v_dev, len(rights) + 1))
    total += before[:, piece * size : (piece + 1) * size]
    cube = masked(total, info, dims, piece * size)
    half = cube.shape[0] // 2
    out[:half] = jnp.concatenate([cube[:half], cube[half:]], axis=2).astype(BF16)
    if out.shape[0] > half:
        out[half:] = jnp.zeros((1, *out.shape[1:]), BF16)


def give(piece, info, dims, mixed, before, rights):
    size = rights[0].shape[1]
    return pl.pallas_call(
        functools.partial(give_kernel, piece),
        out_shape=jax.ShapeDtypeStruct((mixed.shape[0] // 16 + 1 - piece, 8, 2 * size), BF16),
        in_specs=[pl.BlockSpec(memory_space=SMEM)] * 2
        + [pl.BlockSpec(memory_space=VMEM)] * (2 + len(rights)),
        out_specs=pl.BlockSpec(memory_space=VMEM),
        compiler_params=pltpu.CompilerParams(vmem_limit_bytes=24 << 20),
        cost_estimate=SOME,
        name=f"give_{piece}",
    )(info, dims, mixed, before, *rights)


def keep_kernel(info, dims, mixed, before, *refs):
    rights, out = refs[:-1], refs[-1]
    half = len(rights) // 2
    v_dev = rights[0].shape[0]
    blocks = [
        [jnp.concatenate([low[v], high[v]], axis=0) for v in range(v_dev)]
        for low, high in zip(rights[:half], rights[half:])
    ]
    total = before[...] + product(mixed, blocks, others(info, v_dev, half + 1))
    out[0] = masked(total, info, dims, 0).astype(BF16)


def keep(info, dims, mixed, before, rights):
    rows, width = before.shape
    whole = lambda a: pl.BlockSpec(a.shape, lambda i, info, dims, n=a.ndim: (0,) * n)
    return pl.pallas_call(
        keep_kernel,
        out_shape=jax.ShapeDtypeStruct((2, rows // 8, 8, width), BF16),
        grid_spec=pltpu.PrefetchScalarGridSpec(
            num_scalar_prefetch=2,
            grid=(1,),
            in_specs=[whole(a) for a in (mixed, before, *rights)],
            out_specs=pl.BlockSpec(
                (1, rows // 8, 8, width), lambda i, info, dims: (info[3], 0, 0, 0)
            ),
        ),
        compiler_params=pltpu.CompilerParams(vmem_limit_bytes=24 << 20),
        cost_estimate=SMALL,
        name="keep",
    )(info, dims, mixed, before, *rights)


def finish_kernel(info, zero, one, result, out):
    half, _, width = one.shape
    lower = lax.broadcasted_iota(jnp.int32, one.shape, 2) < width // 2

    def halves(ref):
        cube = ref[:half].astype(F32)
        turned = pltpu.roll(cube.reshape(half * 8, width), width // 2, 1)
        return cube, turned.reshape(cube.shape)

    first, first_turned = halves(zero)
    second, second_turned = halves(one)
    out[0, :half] = jnp.where(lower, first, second_turned).astype(BF16)
    out[0, half:] = jnp.where(lower, first_turned, second).astype(BF16)


def finish(info, zero, one, result):
    half, _, width = one.shape
    whole = [pl.BlockSpec(a.shape, lambda i, info: (0, 0, 0)) for a in (zero, one)]
    return pl.pallas_call(
        finish_kernel,
        out_shape=jax.ShapeDtypeStruct(result.shape, BF16),
        grid_spec=pltpu.PrefetchScalarGridSpec(
            num_scalar_prefetch=1,
            grid=(1,),
            in_specs=[*whole, pl.BlockSpec(memory_space=pl.ANY)],
            out_specs=pl.BlockSpec(
                (1, 2 * half, 8, width), lambda i, info: (1 - info[3], 0, 0, 0)
            ),
        ),
        input_output_aliases={3: 0},
        compiler_params=pltpu.CompilerParams(vmem_limit_bytes=16 << 20),
        cost_estimate=SMALL,
        name="finish",
    )(info, zero, one, result)


def after(value, *others):
    return lax.optimization_barrier((value, *others))[0]


def on_device(psi, dims, left_env, right_env, shift, mpo_coef, mpo_mask):
    sec_dev, block, states, width = psi.shape
    w_dev = left_env.shape[0]
    channels = mpo_coef.shape[1]
    groups = lax.axis_size("mpo")
    spots = ("sec", "rep")
    places = lax.axis_size(spots)
    place = lax.axis_index(spots)
    group = lax.axis_index("mpo")
    parity = group % 2
    share = states // groups
    begin_given = ((group + 1 - 2 * parity) * share) // 8 * 8
    begin_kept = (group * share) // 8 * 8
    info = jnp.stack([place, places, group, parity, begin_given, begin_kept]).astype(jnp.int32)

    def swap(block, begin):
        route = []
        for low in range(begin, places - 1, 2):
            route += [(low, low + 1), (low + 1, low)]
        return lax.ppermute(block, spots, route)

    def mirrored(block):
        return lax.ppermute(block, spots, [(i, places - 1 - i) for i in range(places)])

    def beside(block):
        return lax.ppermute(block, "mpo", [(g, g ^ 1) for g in range(groups)])

    steps = range(1, groups)
    far = swap(psi, 1)
    near = swap(psi, 0)
    turned = turn(0, info, dims, psi)
    sent = pack(after(info, turned), mpo_mask, shift, mpo_coef, left_env, groups - 1)
    parcels = [sent[0]] + [ring(p, "mpo", j) for j, p in zip(steps, sent)]
    size = width // 2
    pairs = [(0, (0, width))] + [(j, (r, size)) for r in (0, size) for j in steps]
    entries, rows = [(1 + j) % 2 for j, _ in pairs], [r for _, r in pairs]
    cuts = cut_env(after(info, *sent), right_env, entries, rows)
    passed = [ring(c, "mpo", j) for c, (j, _) in zip(cuts[1:], pairs[1:])]
    turned = turn(1, after(info, *cuts), dims, near, turned)
    same = mirrored(after(cuts[0], turned))
    rights = [mirrored(after(c, turned)) for c in passed]
    turned = turn(2, info, dims, far, turned)
    last = w_dev * block + channels * states
    shifts = jnp.concatenate([p[last, :w_dev] for p in parcels]).astype(jnp.int32)
    given, kept = mix(info, shifts, channels, turned, left_env, parcels)
    given_sum, kept_sum = begin(info, given, kept, same)
    low, high = rights[: groups - 1], rights[groups - 1 :]
    to_give = give(0, after(info, given_sum), dims, given, given_sum, low)
    zero = beside(to_give)
    part = give(1, after(info, given_sum, to_give), dims, given, given_sum, high)
    one = beside(part)
    result = keep(after(info, part), dims, kept, kept_sum, rights)
    result = finish(info, zero, one, result)
    if share != 8:
        result = lax.dynamic_slice_in_dim(result, group * share - begin_kept, share, 2)
    return result


def solution(mesh):
    return jax.shard_map(
        on_device,
        mesh=mesh,
        in_specs=(
            P(("runs", "sec", "rep"), None, None, None),
            P("runs"),
            P("mpo", ("runs", "sec", "rep"), None, None),
            P("mpo", ("runs", "sec", "rep"), None, None),
            P("mpo"),
            P("mpo", None, None, None),
            P("mpo", None),
        ),
        out_specs=P(("runs", "sec", "rep"), None, "mpo", None),
        check_vma=False,
    )
```

```python
import functools

import jax
import jax.numpy as jnp
from jax import lax
from jax.experimental import pallas as pl
from jax.experimental.pallas import tpu as pltpu
from jax.sharding import PartitionSpec as P

F32 = jnp.float32
BF16 = jnp.bfloat16
VMEM = pltpu.VMEM
SMEM = pltpu.SMEM
SMALL = pl.CostEstimate(flops=1 << 10, bytes_accessed=1 << 10, transcendentals=0)
SOME = pl.CostEstimate(flops=1 << 28, bytes_accessed=1 << 20, transcendentals=0)
MORE = pl.CostEstimate(flops=1 << 30, bytes_accessed=1 << 20, transcendentals=0)
PAD = 1


def ring(block, axis, step):
    count = lax.axis_size(axis)
    return lax.ppermute(block, axis, [((i + step) % count, i) for i in range(count)])


def turn_kernel(which, info, dims, psi, *refs):
    turned, plane = refs[-2:]
    _, block, states, width = psi.shape
    place, places = info[0], info[1]
    odd = lax.rem(place, 2)
    home = (place, place + 1 - 2 * odd, place - 1 + 2 * odd)[min(which, 2)]
    entry = slot_of(which, pl.program_id(0), info) % 2
    rows = lax.broadcasted_iota(jnp.int32, (block, width), 0)
    lanes = lax.broadcasted_iota(jnp.int32, (block, width), 1)
    source = jnp.clip(home * 2 + entry, 0, 2 * places - 1)
    keep = (rows < dims[source]) & (lanes < dims[2 * places - 1 - source])
    plane[...] = psi[0].astype(F32).reshape(block * states, width)
    for t in range(states):
        piece = plane[pl.ds(t, block, stride=states), :]
        turned[0, :, t * width : (t + 1) * width] = jnp.where(keep, piece, 0.0).astype(BF16)


def slot_of(which, i, info):
    if which < 2:
        return 2 * which + i
    return 4 + (info[3] if which == 2 else 1 - info[3])


def turn(which, info, dims, psi, *before):
    count, block, states, width = psi.shape
    return pl.pallas_call(
        functools.partial(turn_kernel, which),
        out_shape=jax.ShapeDtypeStruct((6, block, states * width), BF16),
        grid_spec=pltpu.PrefetchScalarGridSpec(
            num_scalar_prefetch=2,
            grid=(count,),
            in_specs=[pl.BlockSpec((1, block, states, width), lambda i, info, dims: (i, 0, 0, 0))]
            + [pl.BlockSpec(memory_space=pl.ANY)] * len(before),
            out_specs=pl.BlockSpec(
                (1, block, states * width),
                lambda i, info, dims: (slot_of(which, i, info), 0, 0),
            ),
            scratch_shapes=[VMEM((block * states, width), F32)],
        ),
        input_output_aliases={3: 0} if before else {},
        compiler_params=pltpu.CompilerParams(vmem_limit_bytes=16 << 20),
        cost_estimate=MORE if which == 2 else SMALL,
        name=f"turn_{which}",
    )(info, dims, psi, *before)


def pack_kernel(info, mask, shift, coef, left, *outs):
    w_dev, channels, states, _ = coef.shape
    block = left.shape[2]
    base = w_dev * block
    lanes = lax.broadcasted_iota(jnp.int32, (states, w_dev * states), 1)
    offsets = jnp.zeros(lanes.shape, F32)
    for w in range(w_dev):
        offsets = jnp.where(lanes == w, shift[w].astype(F32), offsets)
    for j, out in enumerate(outs):
        entry = lax.rem(info[3] + j + 1, 2)
        for w in range(w_dev):
            out[w * block : (w + 1) * block] = left[w, entry]
        for v in range(channels):
            pieces = [coef[w, v].astype(F32) * mask[w, v].astype(F32) for w in range(w_dev)]
            out[base + v * states : base + (v + 1) * states] = jnp.concatenate(
                pieces, axis=1
            ).astype(BF16)
        out[base + channels * states : base + (channels + 1) * states] = offsets.astype(BF16)


def pack(info, mask, shift, coef, left, copies):
    w_dev, channels, states, _ = coef.shape
    rows = w_dev * left.shape[2] + (channels + 1) * states
    return pl.pallas_call(
        pack_kernel,
        out_shape=[jax.ShapeDtypeStruct((rows, w_dev * states), BF16)] * copies,
        in_specs=[pl.BlockSpec(memory_space=SMEM)] * 3 + [pl.BlockSpec(memory_space=VMEM)] * 2,
        out_specs=[pl.BlockSpec(memory_space=VMEM)] * copies,
        compiler_params=pltpu.CompilerParams(vmem_limit_bytes=16 << 20),
        cost_estimate=SMALL,
        name="pack",
    )(info, mask, shift, coef, left)


def cut_psi_kernel(info, psi, out):
    out[0] = psi[info[3]]


def cut_psi(info, psi):
    return pl.pallas_call(
        cut_psi_kernel,
        out_shape=jax.ShapeDtypeStruct((1, *psi.shape[1:]), BF16),
        in_specs=[pl.BlockSpec(memory_space=SMEM), pl.BlockSpec(memory_space=VMEM)],
        out_specs=pl.BlockSpec(memory_space=VMEM),
        compiler_params=pltpu.CompilerParams(vmem_limit_bytes=8 << 20),
        cost_estimate=SMALL,
        name="cut_psi",
    )(info, psi)


def cut_env_kernel(entries, rows, info, env, *outs):
    for entry, (begin, size), out in zip(entries, rows, outs):
        at = lax.rem(info[3] + entry, 2)
        for v in range(env.shape[0]):
            out[v] = env[v, at, begin : begin + size, :]


def cut_env(info, env, entries, rows):
    return pl.pallas_call(
        functools.partial(cut_env_kernel, entries, rows),
        out_shape=[
            jax.ShapeDtypeStruct((env.shape[0], size, env.shape[3]), BF16) for _, size in rows
        ],
        in_specs=[pl.BlockSpec(memory_space=SMEM), pl.BlockSpec(memory_space=VMEM)],
        out_specs=[pl.BlockSpec(memory_space=VMEM)] * len(rows),
        compiler_params=pltpu.CompilerParams(vmem_limit_bytes=8 << 20),
        cost_estimate=SMALL,
        name="cut_env",
    )(info, env)


def mix_kernel(info, shift, *refs):
    turned, own, *parcels = refs[:-4]
    given, kept, first, coupling = refs[-4:]
    groups = len(parcels)
    w_dev, _, block, _ = own.shape
    width = block
    states = turned.shape[2] // width
    channels = coupling.shape[0] // 16
    base = w_dev * block
    place, parity = info[0], info[3]
    near_place = place + 1 - 2 * lax.rem(place, 2)
    sector = place * 2 + parity
    step = block + PAD
    for j, parcel in enumerate(parcels):
        cube = parcel[base : base + channels * states].astype(F32)
        cube = cube.reshape(channels, states, w_dev * states)
        for h in range(2):
            rows = jnp.where(info[4 + h] == 0, cube[:, :8], cube[:, 8:]).reshape(channels * 8, -1)
            coupling[
                h * channels * 8 : (h + 1) * channels * 8,
                j * w_dev * states : (j + 1) * w_dev * states,
            ] = rows.astype(BF16)

    for j, parcel in enumerate(parcels):
        for w in range(w_dev):
            source = sector - shift[j * w_dev + w]
            at = source >> 1
            which = jnp.where(at == place, 0, jnp.where(at == near_place, 1, 2))
            slot = which * 2 + (source & 1)
            matrix = own[w, parity] if j == 0 else parcel[w * block : (w + 1) * block]
            for t in range(0, states, 2):
                product = jnp.dot(
                    matrix,
                    turned[slot, :, t * width : (t + 2) * width],
                    preferred_element_type=F32,
                )
                for h in range(2):
                    row = ((j * w_dev + w) * states + t + h) * step
                    first[pl.ds(row, block), :] = product[:, h * width : (h + 1) * width]

    inner = groups * w_dev * states

    def stage2(i, carry):
        for u in range(4):
            a = i * 8 + u * 2
            pair = [first[pl.ds(a + h, inner, stride=step), :].astype(BF16) for h in range(2)]
            product = jnp.dot(
                coupling[...], jnp.concatenate(pair, axis=1), preferred_element_type=F32
            )
            for half, mixed in enumerate((given, kept)):
                part = product[half * channels * 8 : (half + 1) * channels * 8]
                halves = [
                    part[:, h * width : (h + 1) * width].reshape(channels, 1, 8, width)
                    for h in range(2)
                ]
                both = jnp.concatenate(halves, axis=1).reshape(channels, 16, width).astype(BF16)
                for v in range(channels):
                    mixed[pl.ds(pl.multiple_of(a * 8, 16), 16), v * width : (v + 1) * width] = both[
                        v
                    ]
        return carry

    lax.fori_loop(0, block // 8, stage2, 0, unroll=True)


def mix(info, shift, channels, turned, own, parcels):
    _, block, flat = turned.shape
    width = block
    inner = parcels[0].shape[1] * len(parcels)
    return pl.pallas_call(
        mix_kernel,
        out_shape=[jax.ShapeDtypeStruct((block * 8, channels * width), BF16)] * 2,
        in_specs=[pl.BlockSpec(memory_space=SMEM)] * 2
        + [pl.BlockSpec(memory_space=VMEM)] * (2 + len(parcels)),
        out_specs=[pl.BlockSpec(memory_space=VMEM)] * 2,
        scratch_shapes=[
            VMEM((inner * (block + PAD), width), F32),
            VMEM((channels * 16, inner), BF16),
        ],
        compiler_params=pltpu.CompilerParams(vmem_limit_bytes=(40 if inner <= 256 else 62) << 20),
        cost_estimate=SMALL,
        name="mix",
    )(info, shift, turned, own, *parcels)


def product(mixed, rights, wheres):
    total = None
    for right, where in zip(rights, wheres):
        depth = right[0].shape[1]
        column = pl.multiple_of(where * depth, depth)
        part = lax.dot_general(
            mixed[:, pl.ds(column, len(right) * depth)],
            jnp.concatenate(right, axis=1),
            (((1,), (1,)), ((), ())),
            preferred_element_type=F32,
        )
        total = part if total is None else total + part
    return total


def masked(total, info, dims, begin):
    rows, size = total.shape
    sector = info[0] * 2 + info[3]
    cube = (rows // 8, 8, size)
    a = lax.broadcasted_iota(jnp.int32, cube, 0)
    b = lax.broadcasted_iota(jnp.int32, cube, 2) + begin
    keep = (a < dims[sector]) & (b < dims[2 * info[1] - 1 - sector])
    return jnp.where(keep, total.reshape(cube), 0.0)


def begin_kernel(info, given, kept, low, high, given_out, kept_out):
    v_dev = low.shape[0]
    blocks = [[jnp.concatenate([low[v], high[v]], axis=0) for v in range(v_dev)]]
    given_out[...] = product(given, blocks, [info[2] * v_dev])
    kept_out[...] = product(kept, blocks, [info[2] * v_dev])


def begin(info, given, kept, low, high):
    rows, width = given.shape[0], 2 * low.shape[1]
    return pl.pallas_call(
        begin_kernel,
        out_shape=[jax.ShapeDtypeStruct((rows, width), F32)] * 2,
        in_specs=[pl.BlockSpec(memory_space=SMEM)] + [pl.BlockSpec(memory_space=VMEM)] * 4,
        out_specs=[pl.BlockSpec(memory_space=VMEM)] * 2,
        compiler_params=pltpu.CompilerParams(vmem_limit_bytes=24 << 20),
        cost_estimate=SOME,
        name="begin",
    )(info, given, kept, low, high)


def others(info, v_dev, groups):
    return [lax.rem(info[2] + j, groups) * v_dev for j in range(1, groups)]


def give_kernel(piece, info, dims, mixed, before, *refs):
    rights, out = refs[:-1], refs[-1]
    v_dev, size, _ = rights[0].shape
    blocks = [[right[v] for v in range(v_dev)] for right in rights]
    total = product(mixed, blocks, others(info, v_dev, len(rights) + 1))
    total += before[:, piece * size : (piece + 1) * size]
    cube = masked(total, info, dims, piece * size)
    half = cube.shape[0] // 2
    out[:half] = jnp.concatenate([cube[:half], cube[half:]], axis=2).astype(BF16)
    if out.shape[0] > half:
        out[half:] = jnp.zeros((1, *out.shape[1:]), BF16)


def give(piece, info, dims, mixed, before, rights):
    size = rights[0].shape[1]
    return pl.pallas_call(
        functools.partial(give_kernel, piece),
        out_shape=jax.ShapeDtypeStruct((mixed.shape[0] // 16 + 1 - piece, 8, 2 * size), BF16),
        in_specs=[pl.BlockSpec(memory_space=SMEM)] * 2
        + [pl.BlockSpec(memory_space=VMEM)] * (2 + len(rights)),
        out_specs=pl.BlockSpec(memory_space=VMEM),
        compiler_params=pltpu.CompilerParams(vmem_limit_bytes=24 << 20),
        cost_estimate=SOME,
        name=f"give_{piece}",
    )(info, dims, mixed, before, *rights)


def keep_kernel(info, dims, mixed, before, *refs):
    rights, out = refs[:-1], refs[-1]
    half = len(rights) // 2
    v_dev = rights[0].shape[0]
    blocks = [
        [jnp.concatenate([low[v], high[v]], axis=0) for v in range(v_dev)]
        for low, high in zip(rights[:half], rights[half:])
    ]
    total = before[...] + product(mixed, blocks, others(info, v_dev, half + 1))
    out[0] = masked(total, info, dims, 0).astype(BF16)


def keep(info, dims, mixed, before, rights):
    rows, width = before.shape
    whole = lambda a: pl.BlockSpec(a.shape, lambda i, info, dims, n=a.ndim: (0,) * n)
    return pl.pallas_call(
        keep_kernel,
        out_shape=jax.ShapeDtypeStruct((2, rows // 8, 8, width), BF16),
        grid_spec=pltpu.PrefetchScalarGridSpec(
            num_scalar_prefetch=2,
            grid=(1,),
            in_specs=[whole(a) for a in (mixed, before, *rights)],
            out_specs=pl.BlockSpec(
                (1, rows // 8, 8, width), lambda i, info, dims: (info[3], 0, 0, 0)
            ),
        ),
        compiler_params=pltpu.CompilerParams(vmem_limit_bytes=24 << 20),
        cost_estimate=SMALL,
        name="keep",
    )(info, dims, mixed, before, *rights)


def finish_kernel(info, zero, one, result, out):
    half, _, width = one.shape
    lower = lax.broadcasted_iota(jnp.int32, one.shape, 2) < width // 2

    def halves(ref):
        cube = ref[:half].astype(F32)
        turned = pltpu.roll(cube.reshape(half * 8, width), width // 2, 1)
        return cube, turned.reshape(cube.shape)

    first, first_turned = halves(zero)
    second, second_turned = halves(one)
    out[0, :half] = jnp.where(lower, first, second_turned).astype(BF16)
    out[0, half:] = jnp.where(lower, first_turned, second).astype(BF16)


def finish(info, zero, one, result):
    half, _, width = one.shape
    whole = [pl.BlockSpec(a.shape, lambda i, info: (0, 0, 0)) for a in (zero, one)]
    return pl.pallas_call(
        finish_kernel,
        out_shape=jax.ShapeDtypeStruct(result.shape, BF16),
        grid_spec=pltpu.PrefetchScalarGridSpec(
            num_scalar_prefetch=1,
            grid=(1,),
            in_specs=[*whole, pl.BlockSpec(memory_space=pl.ANY)],
            out_specs=pl.BlockSpec(
                (1, 2 * half, 8, width), lambda i, info: (1 - info[3], 0, 0, 0)
            ),
        ),
        input_output_aliases={3: 0},
        compiler_params=pltpu.CompilerParams(vmem_limit_bytes=16 << 20),
        cost_estimate=SMALL,
        name="finish",
    )(info, zero, one, result)


def after(value, *others):
    return lax.optimization_barrier((value, *others))[0]


def on_device(psi, dims, left_env, right_env, shift, mpo_coef, mpo_mask):
    sec_dev, block, states, width = psi.shape
    w_dev = left_env.shape[0]
    channels = mpo_coef.shape[1]
    groups = lax.axis_size("mpo")
    reps = lax.axis_size("rep")
    spots = ("sec", "rep")
    whole = ("sec", "mpo", "rep")
    places = lax.axis_size(spots)
    place = lax.axis_index(spots)
    group = lax.axis_index("mpo")
    parity = group % 2
    share = states // groups
    begin_given = ((group + 1 - 2 * parity) * share) // 8 * 8
    begin_kept = (group * share) // 8 * 8
    info = jnp.stack([place, places, group, parity, begin_given, begin_kept]).astype(jnp.int32)

    def swap(block, begin):
        route = []
        for low in range(begin, places - 1, 2):
            route += [(low, low + 1), (low + 1, low)]
        return lax.ppermute(block, spots, route)

    def spot(place, group):
        return (place // reps * groups + group) * reps + place % reps

    def cross(block):
        route = []
        for p in range(places):
            for g in range(0, groups, 2):
                source, target = (g + 1, g) if p % 2 == 0 else (g, g + 1)
                route.append((spot(p, source), spot(p, target)))
        return lax.ppermute(block, whole, route)

    def mirrored(block):
        return lax.ppermute(block, spots, [(i, places - 1 - i) for i in range(places)])

    def slanted(block, step):
        route = []
        for p in range(places):
            for g in range(groups):
                route.append((spot(places - 1 - p, (g + step) % groups), spot(p, g)))
        return lax.ppermute(block, whole, route)

    def beside(block):
        return lax.ppermute(block, "mpo", [(g, g ^ 1) for g in range(groups)])

    steps = range(1, groups)
    near = swap(psi, 0)
    one = cut_psi(info, psi)
    early = swap(one, 1)
    turned = turn(1, after(info, one), dims, near)
    size = width // 2
    pairs = [(j, (r, size)) for r in (0, size) for j in range(groups)]
    entries, rows = [(1 + j) % 2 for j, _ in pairs], [r for _, r in pairs]
    cuts = cut_env(after(info, turned), right_env, entries, rows)
    low, high = cuts[:groups], cuts[groups:]
    sent = pack(after(info, *cuts), mpo_mask, shift, mpo_coef, left_env, groups - 1)
    parcels = [sent[0]] + [ring(p, "mpo", j) for j, p in zip(steps, sent)]
    same = [mirrored(low[0]), mirrored(after(high[0], *sent))]
    crossed = cross(after(early, *sent))
    turned = turn(0, after(info, *sent), dims, psi, turned)
    turned = turn(2, after(info, same[0]), dims, early, turned)
    low = [slanted(after(c, turned), j) for c, j in zip(low[1:], steps)]
    high = [slanted(after(c, turned), j) for c, j in zip(high[1:], steps)]
    turned = turn(3, info, dims, crossed, turned)
    last = w_dev * block + channels * states
    shifts = jnp.concatenate([p[last, :w_dev] for p in parcels]).astype(jnp.int32)
    given, kept = mix(info, shifts, channels, turned, left_env, parcels)
    given_sum, kept_sum = begin(info, given, kept, *same)
    to_give = give(0, after(info, given_sum), dims, given, given_sum, low)
    zero = beside(to_give)
    part = give(1, after(info, given_sum, to_give), dims, given, given_sum, high)
    one = beside(part)
    result = keep(after(info, part), dims, kept, kept_sum, low + high)
    result = finish(info, zero, one, result)
    if share != 8:
        result = lax.dynamic_slice_in_dim(result, group * share - begin_kept, share, 2)
    return result


def solution(mesh):
    return jax.shard_map(
        on_device,
        mesh=mesh,
        in_specs=(
            P(("runs", "sec", "rep"), None, None, None),
            P("runs"),
            P("mpo", ("runs", "sec", "rep"), None, None),
            P("mpo", ("runs", "sec", "rep"), None, None),
            P("mpo"),
            P("mpo", None, None, None),
            P("mpo", None),
        ),
        out_specs=P(("runs", "sec", "rep"), None, "mpo", None),
        check_vma=False,
    )
```

```python
import functools

import jax
import jax.numpy as jnp
from jax import lax
from jax.experimental import pallas as pl
from jax.experimental.pallas import tpu as pltpu
from jax.sharding import PartitionSpec as P

F32 = jnp.float32
BF16 = jnp.bfloat16
VMEM = pltpu.VMEM
SMEM = pltpu.SMEM
SMALL = pl.CostEstimate(flops=1 << 10, bytes_accessed=1 << 10, transcendentals=0)
SOME = pl.CostEstimate(flops=1 << 28, bytes_accessed=1 << 20, transcendentals=0)
MORE = pl.CostEstimate(flops=1 << 30, bytes_accessed=1 << 20, transcendentals=0)
PAD = 1


def ring(block, axis, step):
    count = lax.axis_size(axis)
    return lax.ppermute(block, axis, [((i + step) % count, i) for i in range(count)])


def turn_kernel(which, info, dims, psi, *refs):
    turned, plane = refs[-2:]
    _, block, states, width = psi.shape
    place, places = info[0], info[1]
    odd = lax.rem(place, 2)
    home = (place, place + 1 - 2 * odd, place - 1 + 2 * odd)[min(which, 2)]
    entry = slot_of(which, pl.program_id(0), info) % 2
    rows = lax.broadcasted_iota(jnp.int32, (block, width), 0)
    lanes = lax.broadcasted_iota(jnp.int32, (block, width), 1)
    source = jnp.clip(home * 2 + entry, 0, 2 * places - 1)
    keep = (rows < dims[source]) & (lanes < dims[2 * places - 1 - source])
    plane[...] = psi[0].astype(F32).reshape(block * states, width)
    for t in range(states):
        piece = plane[pl.ds(t, block, stride=states), :]
        turned[0, :, t * width : (t + 1) * width] = jnp.where(keep, piece, 0.0).astype(BF16)


def slot_of(which, i, info):
    if which < 2:
        return 2 * which + i
    return 4 + (info[3] if which == 2 else 1 - info[3])


def turn(which, info, dims, psi, *before):
    count, block, states, width = psi.shape
    return pl.pallas_call(
        functools.partial(turn_kernel, which),
        out_shape=jax.ShapeDtypeStruct((6, block, states * width), BF16),
        grid_spec=pltpu.PrefetchScalarGridSpec(
            num_scalar_prefetch=2,
            grid=(count,),
            in_specs=[pl.BlockSpec((1, block, states, width), lambda i, info, dims: (i, 0, 0, 0))]
            + [pl.BlockSpec(memory_space=pl.ANY)] * len(before),
            out_specs=pl.BlockSpec(
                (1, block, states * width),
                lambda i, info, dims: (slot_of(which, i, info), 0, 0),
            ),
            scratch_shapes=[VMEM((block * states, width), F32)],
        ),
        input_output_aliases={3: 0} if before else {},
        compiler_params=pltpu.CompilerParams(vmem_limit_bytes=16 << 20),
        cost_estimate=MORE if which == 2 else SMALL,
        name=f"turn_{which}",
    )(info, dims, psi, *before)


def pack_kernel(info, mask, shift, coef, left, *outs):
    w_dev, channels, states, _ = coef.shape
    block = left.shape[2]
    base = w_dev * block
    lanes = lax.broadcasted_iota(jnp.int32, (states, w_dev * states), 1)
    offsets = jnp.zeros(lanes.shape, F32)
    for w in range(w_dev):
        offsets = jnp.where(lanes == w, shift[w].astype(F32), offsets)
    for j, out in enumerate(outs):
        entry = lax.rem(info[3] + j + 1, 2)
        for w in range(w_dev):
            out[w * block : (w + 1) * block] = left[w, entry]
        for v in range(channels):
            pieces = [coef[w, v].astype(F32) * mask[w, v].astype(F32) for w in range(w_dev)]
            out[base + v * states : base + (v + 1) * states] = jnp.concatenate(
                pieces, axis=1
            ).astype(BF16)
        out[base + channels * states : base + (channels + 1) * states] = offsets.astype(BF16)


def pack(info, mask, shift, coef, left, copies):
    w_dev, channels, states, _ = coef.shape
    rows = w_dev * left.shape[2] + (channels + 1) * states
    return pl.pallas_call(
        pack_kernel,
        out_shape=[jax.ShapeDtypeStruct((rows, w_dev * states), BF16)] * copies,
        in_specs=[pl.BlockSpec(memory_space=SMEM)] * 3 + [pl.BlockSpec(memory_space=VMEM)] * 2,
        out_specs=[pl.BlockSpec(memory_space=VMEM)] * copies,
        compiler_params=pltpu.CompilerParams(vmem_limit_bytes=16 << 20),
        cost_estimate=SMALL,
        name="pack",
    )(info, mask, shift, coef, left)


def cut_psi_kernel(info, psi, out):
    out[0] = psi[info[3]]


def cut_psi(info, psi):
    return pl.pallas_call(
        cut_psi_kernel,
        out_shape=jax.ShapeDtypeStruct((1, *psi.shape[1:]), BF16),
        in_specs=[pl.BlockSpec(memory_space=SMEM), pl.BlockSpec(memory_space=VMEM)],
        out_specs=pl.BlockSpec(memory_space=VMEM),
        compiler_params=pltpu.CompilerParams(vmem_limit_bytes=8 << 20),
        cost_estimate=SMALL,
        name="cut_psi",
    )(info, psi)


def cut_env_kernel(entries, rows, info, env, *outs):
    for entry, (begin, size), out in zip(entries, rows, outs):
        at = lax.rem(info[3] + entry, 2)
        for v in range(env.shape[0]):
            out[v] = env[v, at, begin : begin + size, :]


def cut_env(info, env, entries, rows):
    return pl.pallas_call(
        functools.partial(cut_env_kernel, entries, rows),
        out_shape=[
            jax.ShapeDtypeStruct((env.shape[0], size, env.shape[3]), BF16) for _, size in rows
        ],
        in_specs=[pl.BlockSpec(memory_space=SMEM), pl.BlockSpec(memory_space=VMEM)],
        out_specs=[pl.BlockSpec(memory_space=VMEM)] * len(rows),
        compiler_params=pltpu.CompilerParams(vmem_limit_bytes=8 << 20),
        cost_estimate=SMALL,
        name="cut_env",
    )(info, env)


def mix_kernel(info, shift, *refs):
    turned, own, *parcels = refs[:-4]
    given, kept, first, coupling = refs[-4:]
    groups = len(parcels)
    w_dev, _, block, _ = own.shape
    width = block
    states = turned.shape[2] // width
    channels = coupling.shape[0] // 16
    base = w_dev * block
    place, parity = info[0], info[3]
    near_place = place + 1 - 2 * lax.rem(place, 2)
    sector = place * 2 + parity
    step = block + PAD
    for j, parcel in enumerate(parcels):
        cube = parcel[base : base + channels * states].astype(F32)
        cube = cube.reshape(channels, states, w_dev * states)
        for h in range(2):
            rows = jnp.where(info[4 + h] == 0, cube[:, :8], cube[:, 8:]).reshape(channels * 8, -1)
            coupling[
                h * channels * 8 : (h + 1) * channels * 8,
                j * w_dev * states : (j + 1) * w_dev * states,
            ] = rows.astype(BF16)

    for j, parcel in enumerate(parcels):
        for w in range(w_dev):
            source = sector - shift[j * w_dev + w]
            at = source >> 1
            which = jnp.where(at == place, 0, jnp.where(at == near_place, 1, 2))
            slot = which * 2 + (source & 1)
            matrix = own[w, parity] if j == 0 else parcel[w * block : (w + 1) * block]
            for t in range(0, states, 2):
                product = jnp.dot(
                    matrix,
                    turned[slot, :, t * width : (t + 2) * width],
                    preferred_element_type=F32,
                )
                for h in range(2):
                    row = ((j * w_dev + w) * states + t + h) * step
                    first[pl.ds(row, block), :] = product[:, h * width : (h + 1) * width]

    inner = groups * w_dev * states

    def stage2(i, carry):
        for u in range(4):
            a = i * 8 + u * 2
            pair = [first[pl.ds(a + h, inner, stride=step), :].astype(BF16) for h in range(2)]
            product = jnp.dot(
                coupling[...], jnp.concatenate(pair, axis=1), preferred_element_type=F32
            )
            for half, mixed in enumerate((given, kept)):
                part = product[half * channels * 8 : (half + 1) * channels * 8]
                halves = [
                    part[:, h * width : (h + 1) * width].reshape(channels, 1, 8, width)
                    for h in range(2)
                ]
                both = jnp.concatenate(halves, axis=1).reshape(channels, 16, width).astype(BF16)
                for v in range(channels):
                    mixed[pl.ds(pl.multiple_of(a * 8, 16), 16), v * width : (v + 1) * width] = both[
                        v
                    ]
        return carry

    lax.fori_loop(0, block // 8, stage2, 0, unroll=True)


def mix(info, shift, channels, turned, own, parcels):
    _, block, flat = turned.shape
    width = block
    inner = parcels[0].shape[1] * len(parcels)
    return pl.pallas_call(
        mix_kernel,
        out_shape=[jax.ShapeDtypeStruct((block * 8, channels * width), BF16)] * 2,
        in_specs=[pl.BlockSpec(memory_space=SMEM)] * 2
        + [pl.BlockSpec(memory_space=VMEM)] * (2 + len(parcels)),
        out_specs=[pl.BlockSpec(memory_space=VMEM)] * 2,
        scratch_shapes=[
            VMEM((inner * (block + PAD), width), F32),
            VMEM((channels * 16, inner), BF16),
        ],
        compiler_params=pltpu.CompilerParams(vmem_limit_bytes=(40 if inner <= 256 else 62) << 20),
        cost_estimate=SMALL,
        name="mix",
    )(info, shift, turned, own, *parcels)


def product(mixed, rights, wheres):
    total = None
    for right, where in zip(rights, wheres):
        depth = right[0].shape[1]
        column = pl.multiple_of(where * depth, depth)
        part = lax.dot_general(
            mixed[:, pl.ds(column, len(right) * depth)],
            jnp.concatenate(right, axis=1),
            (((1,), (1,)), ((), ())),
            preferred_element_type=F32,
        )
        total = part if total is None else total + part
    return total


def masked(total, info, dims, begin):
    rows, size = total.shape
    sector = info[0] * 2 + info[3]
    cube = (rows // 8, 8, size)
    a = lax.broadcasted_iota(jnp.int32, cube, 0)
    b = lax.broadcasted_iota(jnp.int32, cube, 2) + begin
    keep = (a < dims[sector]) & (b < dims[2 * info[1] - 1 - sector])
    return jnp.where(keep, total.reshape(cube), 0.0)


def others(info, v_dev, groups):
    return [lax.rem(info[2] + j, groups) * v_dev for j in range(1, groups)]


def spots_of(info, v_dev, count):
    return [info[2] * v_dev] + others(info, v_dev, count)


def give_kernel(piece, info, dims, mixed, *refs):
    rights, out = refs[:-1], refs[-1]
    v_dev, size, _ = rights[0].shape
    blocks = [[right[v] for v in range(v_dev)] for right in rights]
    total = product(mixed, blocks, spots_of(info, v_dev, len(rights)))
    cube = masked(total, info, dims, piece * size)
    half = cube.shape[0] // 2
    out[:half] = jnp.concatenate([cube[:half], cube[half:]], axis=2).astype(BF16)
    if out.shape[0] > half:
        out[half:] = jnp.zeros((1, *out.shape[1:]), BF16)


def give(piece, info, dims, mixed, rights):
    size = rights[0].shape[1]
    return pl.pallas_call(
        functools.partial(give_kernel, piece),
        out_shape=jax.ShapeDtypeStruct((mixed.shape[0] // 16 + 1 - piece, 8, 2 * size), BF16),
        in_specs=[pl.BlockSpec(memory_space=SMEM)] * 2
        + [pl.BlockSpec(memory_space=VMEM)] * (1 + len(rights)),
        out_specs=pl.BlockSpec(memory_space=VMEM),
        compiler_params=pltpu.CompilerParams(vmem_limit_bytes=24 << 20),
        cost_estimate=SOME,
        name=f"give_{piece}",
    )(info, dims, mixed, *rights)


def keep_kernel(info, dims, mixed, *refs):
    rights, out = refs[:-1], refs[-1]
    half = len(rights) // 2
    v_dev = rights[0].shape[0]
    blocks = [
        [jnp.concatenate([low[v], high[v]], axis=0) for v in range(v_dev)]
        for low, high in zip(rights[:half], rights[half:])
    ]
    total = product(mixed, blocks, spots_of(info, v_dev, half))
    out[0] = masked(total, info, dims, 0).astype(BF16)


def keep(info, dims, mixed, rights):
    rows, width = mixed.shape[0], rights[0].shape[2]
    return pl.pallas_call(
        keep_kernel,
        out_shape=jax.ShapeDtypeStruct((2, rows // 8, 8, width), BF16),
        grid_spec=pltpu.PrefetchScalarGridSpec(
            num_scalar_prefetch=2,
            grid=(1,),
            in_specs=[pl.BlockSpec(memory_space=VMEM)] * (1 + len(rights)),
            out_specs=pl.BlockSpec(
                (1, rows // 8, 8, width), lambda i, info, dims: (info[3], 0, 0, 0)
            ),
        ),
        compiler_params=pltpu.CompilerParams(vmem_limit_bytes=24 << 20),
        cost_estimate=SMALL,
        name="keep",
    )(info, dims, mixed, *rights)


def finish_kernel(info, zero, one, result, out):
    half, _, width = one.shape
    lower = lax.broadcasted_iota(jnp.int32, one.shape, 2) < width // 2

    def halves(ref):
        cube = ref[:half].astype(F32)
        turned = pltpu.roll(cube.reshape(half * 8, width), width // 2, 1)
        return cube, turned.reshape(cube.shape)

    first, first_turned = halves(zero)
    second, second_turned = halves(one)
    out[0, :half] = jnp.where(lower, first, second_turned).astype(BF16)
    out[0, half:] = jnp.where(lower, first_turned, second).astype(BF16)


def finish(info, zero, one, result):
    half, _, width = one.shape
    whole = [pl.BlockSpec(a.shape, lambda i, info: (0, 0, 0)) for a in (zero, one)]
    return pl.pallas_call(
        finish_kernel,
        out_shape=jax.ShapeDtypeStruct(result.shape, BF16),
        grid_spec=pltpu.PrefetchScalarGridSpec(
            num_scalar_prefetch=1,
            grid=(1,),
            in_specs=[*whole, pl.BlockSpec(memory_space=pl.ANY)],
            out_specs=pl.BlockSpec(
                (1, 2 * half, 8, width), lambda i, info: (1 - info[3], 0, 0, 0)
            ),
        ),
        input_output_aliases={3: 0},
        compiler_params=pltpu.CompilerParams(vmem_limit_bytes=16 << 20),
        cost_estimate=SMALL,
        name="finish",
    )(info, zero, one, result)


def after(value, *others):
    return lax.optimization_barrier((value, *others))[0]


def on_device(psi, dims, left_env, right_env, shift, mpo_coef, mpo_mask):
    sec_dev, block, states, width = psi.shape
    w_dev = left_env.shape[0]
    channels = mpo_coef.shape[1]
    groups = lax.axis_size("mpo")
    reps = lax.axis_size("rep")
    spots = ("sec", "rep")
    whole = ("sec", "mpo", "rep")
    places = lax.axis_size(spots)
    place = lax.axis_index(spots)
    group = lax.axis_index("mpo")
    parity = group % 2
    share = states // groups
    begin_given = ((group + 1 - 2 * parity) * share) // 8 * 8
    begin_kept = (group * share) // 8 * 8
    info = jnp.stack([place, places, group, parity, begin_given, begin_kept]).astype(jnp.int32)

    def swap(block, begin):
        route = []
        for low in range(begin, places - 1, 2):
            route += [(low, low + 1), (low + 1, low)]
        return lax.ppermute(block, spots, route)

    def spot(place, group):
        return (place // reps * groups + group) * reps + place % reps

    def cross(block):
        route = []
        for p in range(places):
            for g in range(0, groups, 2):
                source, target = (g + 1, g) if p % 2 == 0 else (g, g + 1)
                route.append((spot(p, source), spot(p, target)))
        return lax.ppermute(block, whole, route)

    def mirrored(block):
        return lax.ppermute(block, spots, [(i, places - 1 - i) for i in range(places)])

    def slanted(block, step):
        route = []
        for p in range(places):
            for g in range(groups):
                route.append((spot(places - 1 - p, (g + step) % groups), spot(p, g)))
        return lax.ppermute(block, whole, route)

    def beside(block):
        return lax.ppermute(block, "mpo", [(g, g ^ 1) for g in range(groups)])

    steps = range(1, groups)
    near = swap(psi, 0)
    one = cut_psi(info, psi)
    early = swap(one, 1)
    turned = turn(1, after(info, one), dims, near)
    size = width // 2
    pairs = [(j, (r, size)) for r in (0, size) for j in range(groups)]
    entries, rows = [(1 + j) % 2 for j, _ in pairs], [r for _, r in pairs]
    cuts = cut_env(after(info, turned), right_env, entries, rows)
    low, high = cuts[:groups], cuts[groups:]
    sent = pack(after(info, *cuts), mpo_mask, shift, mpo_coef, left_env, groups - 1)
    parcels = [sent[0]] + [ring(p, "mpo", j) for j, p in zip(steps, sent)]
    passed = [ring(c, "mpo", j) for c, j in zip(high[1:], steps)]
    same = [mirrored(low[0]), mirrored(after(high[0], *sent))]
    crossed = cross(after(early, *sent))
    turned = turn(0, after(info, *sent), dims, psi, turned)
    turned = turn(2, after(info, same[0]), dims, early, turned)
    low = [slanted(after(c, turned), j) for c, j in zip(low[1:], steps)]
    high = [mirrored(after(p, turned)) for p in passed]
    turned = turn(3, info, dims, crossed, turned)
    last = w_dev * block + channels * states
    shifts = jnp.concatenate([p[last, :w_dev] for p in parcels]).astype(jnp.int32)
    given, kept = mix(info, shifts, channels, turned, left_env, parcels)
    low, high = [same[0], *low], [same[1], *high]
    to_give = give(0, info, dims, given, low)
    zero = beside(to_give)
    part = give(1, after(info, to_give), dims, given, high)
    one = beside(part)
    result = keep(after(info, part), dims, kept, low + high)
    result = finish(info, zero, one, result)
    if share != 8:
        result = lax.dynamic_slice_in_dim(result, group * share - begin_kept, share, 2)
    return result


def solution(mesh):
    return jax.shard_map(
        on_device,
        mesh=mesh,
        in_specs=(
            P(("runs", "sec", "rep"), None, None, None),
            P("runs"),
            P("mpo", ("runs", "sec", "rep"), None, None),
            P("mpo", ("runs", "sec", "rep"), None, None),
            P("mpo"),
            P("mpo", None, None, None),
            P("mpo", None),
        ),
        out_specs=P(("runs", "sec", "rep"), None, "mpo", None),
        check_vma=False,
    )
```

```python
import functools

import jax
import jax.numpy as jnp
from jax import lax
from jax.experimental import pallas as pl
from jax.experimental.pallas import tpu as pltpu
from jax.sharding import PartitionSpec as P

F32 = jnp.float32
BF16 = jnp.bfloat16
VMEM = pltpu.VMEM
SMEM = pltpu.SMEM
SMALL = pl.CostEstimate(flops=1 << 10, bytes_accessed=1 << 10, transcendentals=0)
SOME = pl.CostEstimate(flops=1 << 28, bytes_accessed=1 << 20, transcendentals=0)
MORE = pl.CostEstimate(flops=1 << 30, bytes_accessed=1 << 20, transcendentals=0)
PAD = 1


def ring(block, axis, step):
    count = lax.axis_size(axis)
    return lax.ppermute(block, axis, [((i + step) % count, i) for i in range(count)])


def turn_kernel(which, info, dims, psi, *refs):
    turned, plane = refs[-2:]
    _, block, states, width = psi.shape
    place, places = info[0], info[1]
    odd = lax.rem(place, 2)
    home = (place, place + 1 - 2 * odd, place - 1 + 2 * odd)[min(which, 2)]
    entry = slot_of(which, pl.program_id(0), info) % 2
    rows = lax.broadcasted_iota(jnp.int32, (block, width), 0)
    lanes = lax.broadcasted_iota(jnp.int32, (block, width), 1)
    source = jnp.clip(home * 2 + entry, 0, 2 * places - 1)
    keep = (rows < dims[source]) & (lanes < dims[2 * places - 1 - source])
    plane[: block * states] = psi[0].astype(F32).reshape(block * states, width)
    for t in range(states):
        piece = plane[pl.ds(t, block, stride=states), :]
        turned[0, :, t * width : (t + 1) * width] = jnp.where(keep, piece, 0.0).astype(BF16)


def slot_of(which, i, info):
    if which < 2:
        return 2 * which + i
    return 4 + (info[3] if which == 2 else 1 - info[3])


def turn(which, info, dims, psi, *before):
    count, block, states, width = psi.shape
    return pl.pallas_call(
        functools.partial(turn_kernel, which),
        out_shape=jax.ShapeDtypeStruct((6, block, states * width), BF16),
        grid_spec=pltpu.PrefetchScalarGridSpec(
            num_scalar_prefetch=2,
            grid=(count,),
            in_specs=[pl.BlockSpec((1, block, states, width), lambda i, info, dims: (i, 0, 0, 0))]
            + [pl.BlockSpec(memory_space=pl.ANY)] * len(before),
            out_specs=pl.BlockSpec(
                (1, block, states * width),
                lambda i, info, dims: (slot_of(which, i, info), 0, 0),
            ),
            scratch_shapes=[VMEM(((block + 1) * states, width), F32)],
        ),
        input_output_aliases={3: 0} if before else {},
        compiler_params=pltpu.CompilerParams(vmem_limit_bytes=16 << 20),
        cost_estimate=MORE if which == 2 else SMALL,
        name=f"turn_{which}",
    )(info, dims, psi, *before)


def pack_kernel(info, mask, shift, coef, left, *outs):
    w_dev, channels, states, _ = coef.shape
    block = left.shape[2]
    base = w_dev * block
    lanes = lax.broadcasted_iota(jnp.int32, (states, w_dev * states), 1)
    offsets = jnp.zeros(lanes.shape, F32)
    for w in range(w_dev):
        offsets = jnp.where(lanes == w, shift[w].astype(F32), offsets)
    for j, out in enumerate(outs):
        entry = lax.rem(info[3] + j + 1, 2)
        for w in range(w_dev):
            out[w * block : (w + 1) * block] = left[w, entry]
        for v in range(channels):
            pieces = [coef[w, v].astype(F32) * mask[w, v].astype(F32) for w in range(w_dev)]
            out[base + v * states : base + (v + 1) * states] = jnp.concatenate(
                pieces, axis=1
            ).astype(BF16)
        out[base + channels * states : base + (channels + 1) * states] = offsets.astype(BF16)


def pack(info, mask, shift, coef, left, copies):
    w_dev, channels, states, _ = coef.shape
    rows = w_dev * left.shape[2] + (channels + 1) * states
    return pl.pallas_call(
        pack_kernel,
        out_shape=[jax.ShapeDtypeStruct((rows, w_dev * states), BF16)] * copies,
        in_specs=[pl.BlockSpec(memory_space=SMEM)] * 3 + [pl.BlockSpec(memory_space=VMEM)] * 2,
        out_specs=[pl.BlockSpec(memory_space=VMEM)] * copies,
        compiler_params=pltpu.CompilerParams(vmem_limit_bytes=16 << 20),
        cost_estimate=SMALL,
        name="pack",
    )(info, mask, shift, coef, left)


def cut_psi_kernel(info, psi, out):
    out[0] = psi[info[3]]


def cut_psi(info, psi):
    return pl.pallas_call(
        cut_psi_kernel,
        out_shape=jax.ShapeDtypeStruct((1, *psi.shape[1:]), BF16),
        in_specs=[pl.BlockSpec(memory_space=SMEM), pl.BlockSpec(memory_space=VMEM)],
        out_specs=pl.BlockSpec(memory_space=VMEM),
        compiler_params=pltpu.CompilerParams(vmem_limit_bytes=8 << 20),
        cost_estimate=SMALL,
        name="cut_psi",
    )(info, psi)


def cut_env_kernel(entries, rows, info, env, *outs):
    for entry, (begin, size), out in zip(entries, rows, outs):
        at = lax.rem(info[3] + entry, 2)
        for v in range(env.shape[0]):
            out[v] = env[v, at, begin : begin + size, :]


def cut_env(info, env, entries, rows):
    return pl.pallas_call(
        functools.partial(cut_env_kernel, entries, rows),
        out_shape=[
            jax.ShapeDtypeStruct((env.shape[0], size, env.shape[3]), BF16) for _, size in rows
        ],
        in_specs=[pl.BlockSpec(memory_space=SMEM), pl.BlockSpec(memory_space=VMEM)],
        out_specs=[pl.BlockSpec(memory_space=VMEM)] * len(rows),
        compiler_params=pltpu.CompilerParams(vmem_limit_bytes=8 << 20),
        cost_estimate=SMALL,
        name="cut_env",
    )(info, env)


def mix_kernel(info, shift, *refs):
    turned, own, *parcels = refs[:-4]
    given, kept, first, coupling = refs[-4:]
    groups = len(parcels)
    w_dev, _, block, _ = own.shape
    width = block
    states = turned.shape[2] // width
    channels = coupling.shape[0] // 16
    base = w_dev * block
    place, parity = info[0], info[3]
    near_place = place + 1 - 2 * lax.rem(place, 2)
    sector = place * 2 + parity
    step = block + PAD
    for j, parcel in enumerate(parcels):
        cube = parcel[base : base + channels * states].astype(F32)
        cube = cube.reshape(channels, states, w_dev * states)
        for h in range(2):
            rows = jnp.where(info[4 + h] == 0, cube[:, :8], cube[:, 8:]).reshape(channels * 8, -1)
            coupling[
                h * channels * 8 : (h + 1) * channels * 8,
                j * w_dev * states : (j + 1) * w_dev * states,
            ] = rows.astype(BF16)

    for j, parcel in enumerate(parcels):
        for w in range(w_dev):
            source = sector - shift[j * w_dev + w]
            at = source >> 1
            which = jnp.where(at == place, 0, jnp.where(at == near_place, 1, 2))
            slot = which * 2 + (source & 1)
            matrix = own[w, parity] if j == 0 else parcel[w * block : (w + 1) * block]
            for t in range(0, states, 2):
                product = jnp.dot(
                    matrix,
                    turned[slot, :, t * width : (t + 2) * width],
                    preferred_element_type=F32,
                )
                for h in range(2):
                    row = ((j * w_dev + w) * states + t + h) * step
                    first[pl.ds(row, block), :] = product[:, h * width : (h + 1) * width]

    inner = groups * w_dev * states

    def stage2(i, carry):
        for u in range(4):
            a = i * 8 + u * 2
            pair = [first[pl.ds(a + h, inner, stride=step), :].astype(BF16) for h in range(2)]
            product = jnp.dot(
                coupling[...], jnp.concatenate(pair, axis=1), preferred_element_type=F32
            )
            for half, mixed in enumerate((given, kept)):
                part = product[half * channels * 8 : (half + 1) * channels * 8]
                halves = [
                    part[:, h * width : (h + 1) * width].reshape(channels, 1, 8, width)
                    for h in range(2)
                ]
                both = jnp.concatenate(halves, axis=1).reshape(channels, 16, width).astype(BF16)
                for v in range(channels):
                    mixed[pl.ds(pl.multiple_of(a * 8, 16), 16), v * width : (v + 1) * width] = both[
                        v
                    ]
        return carry

    lax.fori_loop(0, block // 8, stage2, 0, unroll=True)


def mix(info, shift, channels, turned, own, parcels):
    _, block, flat = turned.shape
    width = block
    inner = parcels[0].shape[1] * len(parcels)
    return pl.pallas_call(
        mix_kernel,
        out_shape=[jax.ShapeDtypeStruct((block * 8, channels * width), BF16)] * 2,
        in_specs=[pl.BlockSpec(memory_space=SMEM)] * 2
        + [pl.BlockSpec(memory_space=VMEM)] * (2 + len(parcels)),
        out_specs=[pl.BlockSpec(memory_space=VMEM)] * 2,
        scratch_shapes=[
            VMEM(((inner + 1) * (block + PAD) + 7, width), F32),
            VMEM((channels * 16, inner), BF16),
        ],
        compiler_params=pltpu.CompilerParams(vmem_limit_bytes=(40 if inner <= 256 else 62) << 20),
        cost_estimate=SMALL,
        name="mix",
    )(info, shift, turned, own, *parcels)


def product(mixed, rights, wheres):
    total = None
    for right, where in zip(rights, wheres):
        depth = right[0].shape[1]
        column = pl.multiple_of(where * depth, depth)
        part = lax.dot_general(
            mixed[:, pl.ds(column, len(right) * depth)],
            jnp.concatenate(right, axis=1),
            (((1,), (1,)), ((), ())),
            preferred_element_type=F32,
        )
        total = part if total is None else total + part
    return total


def masked(total, info, dims, begin):
    rows, size = total.shape
    sector = info[0] * 2 + info[3]
    cube = (rows // 8, 8, size)
    a = lax.broadcasted_iota(jnp.int32, cube, 0)
    b = lax.broadcasted_iota(jnp.int32, cube, 2) + begin
    keep = (a < dims[sector]) & (b < dims[2 * info[1] - 1 - sector])
    return jnp.where(keep, total.reshape(cube), 0.0)


def begin_kernel(info, given, kept, low, high, given_out, kept_out):
    v_dev = low.shape[0]
    blocks = [[jnp.concatenate([low[v], high[v]], axis=0) for v in range(v_dev)]]
    given_out[...] = product(given, blocks, [info[2] * v_dev])
    kept_out[...] = product(kept, blocks, [info[2] * v_dev])


def begin(info, given, kept, low, high):
    rows, width = given.shape[0], 2 * low.shape[1]
    return pl.pallas_call(
        begin_kernel,
        out_shape=[jax.ShapeDtypeStruct((rows, width), F32)] * 2,
        in_specs=[pl.BlockSpec(memory_space=SMEM)] + [pl.BlockSpec(memory_space=VMEM)] * 4,
        out_specs=[pl.BlockSpec(memory_space=VMEM)] * 2,
        compiler_params=pltpu.CompilerParams(vmem_limit_bytes=24 << 20),
        cost_estimate=SOME,
        name="begin",
    )(info, given, kept, low, high)


def others(info, v_dev, groups):
    return [lax.rem(info[2] + j, groups) * v_dev for j in range(1, groups)]


def give_kernel(piece, info, dims, mixed, before, *refs):
    rights, out = refs[:-1], refs[-1]
    v_dev, size, _ = rights[0].shape
    blocks = [[right[v] for v in range(v_dev)] for right in rights]
    total = product(mixed, blocks, others(info, v_dev, len(rights) + 1))
    total += before[:, piece * size : (piece + 1) * size]
    cube = masked(total, info, dims, piece * size)
    half = cube.shape[0] // 2
    out[:half] = jnp.concatenate([cube[:half], cube[half:]], axis=2).astype(BF16)
    if out.shape[0] > half:
        out[half:] = jnp.zeros((1, *out.shape[1:]), BF16)


def give(piece, info, dims, mixed, before, rights):
    size = rights[0].shape[1]
    return pl.pallas_call(
        functools.partial(give_kernel, piece),
        out_shape=jax.ShapeDtypeStruct((mixed.shape[0] // 16 + 1 - piece, 8, 2 * size), BF16),
        in_specs=[pl.BlockSpec(memory_space=SMEM)] * 2
        + [pl.BlockSpec(memory_space=VMEM)] * (2 + len(rights)),
        out_specs=pl.BlockSpec(memory_space=VMEM),
        compiler_params=pltpu.CompilerParams(vmem_limit_bytes=24 << 20),
        cost_estimate=SOME,
        name=f"give_{piece}",
    )(info, dims, mixed, before, *rights)


def keep_kernel(info, dims, mixed, before, *refs):
    rights, out = refs[:-1], refs[-1]
    half = len(rights) // 2
    v_dev = rights[0].shape[0]
    blocks = [
        [jnp.concatenate([low[v], high[v]], axis=0) for v in range(v_dev)]
        for low, high in zip(rights[:half], rights[half:])
    ]
    total = before[...] + product(mixed, blocks, others(info, v_dev, half + 1))
    out[0] = masked(total, info, dims, 0).astype(BF16)


def keep(info, dims, mixed, before, rights):
    rows, width = before.shape
    whole = lambda a: pl.BlockSpec(a.shape, lambda i, info, dims, n=a.ndim: (0,) * n)
    return pl.pallas_call(
        keep_kernel,
        out_shape=jax.ShapeDtypeStruct((2, rows // 8, 8, width), BF16),
        grid_spec=pltpu.PrefetchScalarGridSpec(
            num_scalar_prefetch=2,
            grid=(1,),
            in_specs=[whole(a) for a in (mixed, before, *rights)],
            out_specs=pl.BlockSpec(
                (1, rows // 8, 8, width), lambda i, info, dims: (info[3], 0, 0, 0)
            ),
        ),
        compiler_params=pltpu.CompilerParams(vmem_limit_bytes=24 << 20),
        cost_estimate=SMALL,
        name="keep",
    )(info, dims, mixed, before, *rights)


def finish_kernel(info, zero, one, result, out):
    half, _, width = one.shape
    lower = lax.broadcasted_iota(jnp.int32, one.shape, 2) < width // 2

    def halves(ref):
        cube = ref[:half].astype(F32)
        turned = pltpu.roll(cube.reshape(half * 8, width), width // 2, 1)
        return cube, turned.reshape(cube.shape)

    first, first_turned = halves(zero)
    second, second_turned = halves(one)
    out[0, :half] = jnp.where(lower, first, second_turned).astype(BF16)
    out[0, half:] = jnp.where(lower, first_turned, second).astype(BF16)


def finish(info, zero, one, result):
    half, _, width = one.shape
    whole = [pl.BlockSpec(a.shape, lambda i, info: (0, 0, 0)) for a in (zero, one)]
    return pl.pallas_call(
        finish_kernel,
        out_shape=jax.ShapeDtypeStruct(result.shape, BF16),
        grid_spec=pltpu.PrefetchScalarGridSpec(
            num_scalar_prefetch=1,
            grid=(1,),
            in_specs=[*whole, pl.BlockSpec(memory_space=pl.ANY)],
            out_specs=pl.BlockSpec(
                (1, 2 * half, 8, width), lambda i, info: (1 - info[3], 0, 0, 0)
            ),
        ),
        input_output_aliases={3: 0},
        compiler_params=pltpu.CompilerParams(vmem_limit_bytes=16 << 20),
        cost_estimate=SMALL,
        name="finish",
    )(info, zero, one, result)


def after(value, *others):
    return lax.optimization_barrier((value, *others))[0]


def on_device(psi, dims, left_env, right_env, shift, mpo_coef, mpo_mask):
    sec_dev, block, states, width = psi.shape
    w_dev = left_env.shape[0]
    channels = mpo_coef.shape[1]
    groups = lax.axis_size("mpo")
    reps = lax.axis_size("rep")
    spots = ("sec", "rep")
    whole = ("sec", "mpo", "rep")
    places = lax.axis_size(spots)
    place = lax.axis_index(spots)
    group = lax.axis_index("mpo")
    parity = group % 2
    share = states // groups
    begin_given = ((group + 1 - 2 * parity) * share) // 8 * 8
    begin_kept = (group * share) // 8 * 8
    info = jnp.stack([place, places, group, parity, begin_given, begin_kept]).astype(jnp.int32)

    def swap(block, begin):
        route = []
        for low in range(begin, places - 1, 2):
            route += [(low, low + 1), (low + 1, low)]
        return lax.ppermute(block, spots, route)

    def spot(place, group):
        return (place // reps * groups + group) * reps + place % reps

    def cross(block):
        route = []
        for p in range(places):
            for g in range(0, groups, 2):
                source, target = (g + 1, g) if p % 2 == 0 else (g, g + 1)
                route.append((spot(p, source), spot(p, target)))
        return lax.ppermute(block, whole, route)

    def mirrored(block):
        return lax.ppermute(block, spots, [(i, places - 1 - i) for i in range(places)])

    def slanted(block, step):
        route = []
        for p in range(places):
            for g in range(groups):
                route.append((spot(places - 1 - p, (g + step) % groups), spot(p, g)))
        return lax.ppermute(block, whole, route)

    def beside(block):
        return lax.ppermute(block, "mpo", [(g, g ^ 1) for g in range(groups)])

    steps = range(1, groups)
    near = swap(psi, 0)
    one = cut_psi(info, psi)
    early = swap(one, 1)
    turned = turn(1, after(info, one), dims, near)
    size = width // 2
    pairs = [(j, (r, size)) for r in (0, size) for j in range(groups)]
    entries, rows = [(1 + j) % 2 for j, _ in pairs], [r for _, r in pairs]
    cuts = cut_env(after(info, turned), right_env, entries, rows)
    low, high = cuts[:groups], cuts[groups:]
    sent = pack(after(info, *cuts), mpo_mask, shift, mpo_coef, left_env, groups - 1)
    parcels = [sent[0]] + [ring(p, "mpo", j) for j, p in zip(steps, sent)]
    same = [mirrored(low[0]), mirrored(after(high[0], *sent))]
    crossed = cross(after(early, *sent))
    turned = turn(0, after(info, *sent), dims, psi, turned)
    turned = turn(2, after(info, same[0]), dims, early, turned)
    low = [slanted(after(c, turned), j) for c, j in zip(low[1:], steps)]
    high = [slanted(after(c, turned), j) for c, j in zip(high[1:], steps)]
    turned = turn(3, info, dims, crossed, turned)
    last = w_dev * block + channels * states
    shifts = jnp.concatenate([p[last, :w_dev] for p in parcels]).astype(jnp.int32)
    given, kept = mix(info, shifts, channels, turned, left_env, parcels)
    given_sum, kept_sum = begin(info, given, kept, *same)
    to_give = give(0, after(info, given_sum), dims, given, given_sum, low)
    zero = beside(to_give)
    part = give(1, after(info, given_sum, to_give), dims, given, given_sum, high)
    one = beside(part)
    result = keep(after(info, part), dims, kept, kept_sum, low + high)
    result = finish(info, zero, one, result)
    if share != 8:
        result = lax.dynamic_slice_in_dim(result, group * share - begin_kept, share, 2)
    return result


def solution(mesh):
    return jax.shard_map(
        on_device,
        mesh=mesh,
        in_specs=(
            P(("runs", "sec", "rep"), None, None, None),
            P("runs"),
            P("mpo", ("runs", "sec", "rep"), None, None),
            P("mpo", ("runs", "sec", "rep"), None, None),
            P("mpo"),
            P("mpo", None, None, None),
            P("mpo", None),
        ),
        out_specs=P(("runs", "sec", "rep"), None, "mpo", None),
        check_vma=False,
    )
```

```python
import functools

import jax
import jax.numpy as jnp
from jax import lax
from jax.experimental import pallas as pl
from jax.experimental.pallas import tpu as pltpu
from jax.sharding import PartitionSpec as P

F32 = jnp.float32
BF16 = jnp.bfloat16
VMEM = pltpu.VMEM
SMEM = pltpu.SMEM
SMALL = pl.CostEstimate(flops=1 << 10, bytes_accessed=1 << 10, transcendentals=0)
SOME = pl.CostEstimate(flops=1 << 28, bytes_accessed=1 << 20, transcendentals=0)
MORE = pl.CostEstimate(flops=1 << 30, bytes_accessed=1 << 20, transcendentals=0)
PAD = 1


def ring(block, axis, step):
    count = lax.axis_size(axis)
    return lax.ppermute(block, axis, [((i + step) % count, i) for i in range(count)])


def turn_kernel(which, info, dims, psi, *refs):
    turned, plane = refs[-2:]
    _, block, states, width = psi.shape
    place, places = info[0], info[1]
    odd = lax.rem(place, 2)
    home = (place, place + 1 - 2 * odd, place - 1 + 2 * odd)[min(which, 2)]
    entry = slot_of(which, pl.program_id(0), info) % 2
    rows = lax.broadcasted_iota(jnp.int32, (block, width), 0)
    lanes = lax.broadcasted_iota(jnp.int32, (block, width), 1)
    source = jnp.clip(home * 2 + entry, 0, 2 * places - 1)
    keep = (rows < dims[source]) & (lanes < dims[2 * places - 1 - source])
    plane[: block * states] = psi[0].astype(F32).reshape(block * states, width)
    for t in range(states):
        piece = plane[pl.ds(t, block, stride=states), :]
        turned[0, :, t * width : (t + 1) * width] = jnp.where(keep, piece, 0.0).astype(BF16)


def slot_of(which, i, info):
    if which < 2:
        return 2 * which + i
    return 4 + (info[3] if which == 2 else 1 - info[3])


def turn(which, info, dims, psi, *before):
    count, block, states, width = psi.shape
    return pl.pallas_call(
        functools.partial(turn_kernel, which),
        out_shape=jax.ShapeDtypeStruct((6, block, states * width), BF16),
        grid_spec=pltpu.PrefetchScalarGridSpec(
            num_scalar_prefetch=2,
            grid=(count,),
            in_specs=[pl.BlockSpec((1, block, states, width), lambda i, info, dims: (i, 0, 0, 0))]
            + [pl.BlockSpec(memory_space=pl.ANY)] * len(before),
            out_specs=pl.BlockSpec(
                (1, block, states * width),
                lambda i, info, dims: (slot_of(which, i, info), 0, 0),
            ),
            scratch_shapes=[VMEM(((block + 1) * states, width), F32)],
        ),
        input_output_aliases={3: 0} if before else {},
        compiler_params=pltpu.CompilerParams(vmem_limit_bytes=16 << 20),
        cost_estimate=MORE if which == 2 else SMALL,
        name=f"turn_{which}",
    )(info, dims, psi, *before)


def pack_kernel(info, mask, shift, coef, left, *outs):
    w_dev, channels, states, _ = coef.shape
    block = left.shape[2]
    base = w_dev * block
    lanes = lax.broadcasted_iota(jnp.int32, (states, w_dev * states), 1)
    offsets = jnp.zeros(lanes.shape, F32)
    for w in range(w_dev):
        offsets = jnp.where(lanes == w, shift[w].astype(F32), offsets)
    for j, out in enumerate(outs):
        entry = lax.rem(info[3] + j + 1, 2)
        for w in range(w_dev):
            out[w * block : (w + 1) * block] = left[w, entry]
        for v in range(channels):
            pieces = [coef[w, v].astype(F32) * mask[w, v].astype(F32) for w in range(w_dev)]
            out[base + v * states : base + (v + 1) * states] = jnp.concatenate(
                pieces, axis=1
            ).astype(BF16)
        out[base + channels * states : base + (channels + 1) * states] = offsets.astype(BF16)


def pack(info, mask, shift, coef, left, copies):
    w_dev, channels, states, _ = coef.shape
    rows = w_dev * left.shape[2] + (channels + 1) * states
    return pl.pallas_call(
        pack_kernel,
        out_shape=[jax.ShapeDtypeStruct((rows, w_dev * states), BF16)] * copies,
        in_specs=[pl.BlockSpec(memory_space=SMEM)] * 3 + [pl.BlockSpec(memory_space=VMEM)] * 2,
        out_specs=[pl.BlockSpec(memory_space=VMEM)] * copies,
        compiler_params=pltpu.CompilerParams(vmem_limit_bytes=16 << 20),
        cost_estimate=SMALL,
        name="pack",
    )(info, mask, shift, coef, left)


def cut_psi_kernel(info, psi, out):
    out[0] = psi[info[3]]


def cut_psi(info, psi):
    return pl.pallas_call(
        cut_psi_kernel,
        out_shape=jax.ShapeDtypeStruct((1, *psi.shape[1:]), BF16),
        in_specs=[pl.BlockSpec(memory_space=SMEM), pl.BlockSpec(memory_space=VMEM)],
        out_specs=pl.BlockSpec(memory_space=VMEM),
        compiler_params=pltpu.CompilerParams(vmem_limit_bytes=8 << 20),
        cost_estimate=SMALL,
        name="cut_psi",
    )(info, psi)


def cut_env_kernel(entries, rows, info, env, *outs):
    for entry, (begin, size), out in zip(entries, rows, outs):
        at = lax.rem(info[3] + entry, 2)
        for v in range(env.shape[0]):
            out[v] = env[v, at, begin : begin + size, :]


def cut_env(info, env, entries, rows):
    return pl.pallas_call(
        functools.partial(cut_env_kernel, entries, rows),
        out_shape=[
            jax.ShapeDtypeStruct((env.shape[0], size, env.shape[3]), BF16) for _, size in rows
        ],
        in_specs=[pl.BlockSpec(memory_space=SMEM), pl.BlockSpec(memory_space=VMEM)],
        out_specs=[pl.BlockSpec(memory_space=VMEM)] * len(rows),
        compiler_params=pltpu.CompilerParams(vmem_limit_bytes=8 << 20),
        cost_estimate=SMALL,
        name="cut_env",
    )(info, env)


def mix_kernel(info, shift, *refs):
    turned, own, *parcels = refs[:-4]
    given, kept, first, coupling = refs[-4:]
    groups = len(parcels)
    w_dev, _, block, _ = own.shape
    width = block
    states = turned.shape[2] // width
    channels = coupling.shape[0] // 16
    base = w_dev * block
    place, parity = info[0], info[3]
    near_place = place + 1 - 2 * lax.rem(place, 2)
    sector = place * 2 + parity
    step = block + PAD
    for j, parcel in enumerate(parcels):
        cube = parcel[base : base + channels * states].astype(F32)
        cube = cube.reshape(channels, states, w_dev * states)
        for h in range(2):
            rows = jnp.where(info[4 + h] == 0, cube[:, :8], cube[:, 8:]).reshape(channels * 8, -1)
            coupling[
                h * channels * 8 : (h + 1) * channels * 8,
                j * w_dev * states : (j + 1) * w_dev * states,
            ] = rows.astype(BF16)

    for j, parcel in enumerate(parcels):
        for w in range(w_dev):
            source = sector - shift[j * w_dev + w]
            at = source >> 1
            which = jnp.where(at == place, 0, jnp.where(at == near_place, 1, 2))
            slot = which * 2 + (source & 1)
            matrix = own[w, parity] if j == 0 else parcel[w * block : (w + 1) * block]
            for t in range(0, states, 2):
                product = jnp.dot(
                    matrix,
                    turned[slot, :, t * width : (t + 2) * width],
                    preferred_element_type=F32,
                )
                for h in range(2):
                    row = ((j * w_dev + w) * states + t + h) * step
                    first[pl.ds(row, block), :] = product[:, h * width : (h + 1) * width]

    inner = groups * w_dev * states

    def stage2(i, carry):
        for u in range(4):
            a = i * 8 + u * 2
            pair = [first[pl.ds(a + h, inner, stride=step), :].astype(BF16) for h in range(2)]
            product = jnp.dot(
                coupling[...], jnp.concatenate(pair, axis=1), preferred_element_type=F32
            )
            for half, mixed in enumerate((given, kept)):
                part = product[half * channels * 8 : (half + 1) * channels * 8]
                halves = [
                    part[:, h * width : (h + 1) * width].reshape(channels, 1, 8, width)
                    for h in range(2)
                ]
                both = jnp.concatenate(halves, axis=1).reshape(channels, 16, width).astype(BF16)
                for v in range(channels):
                    mixed[pl.ds(pl.multiple_of(a * 8, 16), 16), v * width : (v + 1) * width] = both[
                        v
                    ]
        return carry

    lax.fori_loop(0, block // 8, stage2, 0, unroll=True)


def mix(info, shift, channels, turned, own, parcels):
    _, block, flat = turned.shape
    width = block
    inner = parcels[0].shape[1] * len(parcels)
    return pl.pallas_call(
        mix_kernel,
        out_shape=[jax.ShapeDtypeStruct((block * 8, channels * width), BF16)] * 2,
        in_specs=[pl.BlockSpec(memory_space=SMEM)] * 2
        + [pl.BlockSpec(memory_space=VMEM)] * (2 + len(parcels)),
        out_specs=[pl.BlockSpec(memory_space=VMEM)] * 2,
        scratch_shapes=[
            VMEM(((inner + 1) * (block + PAD) + 7, width), F32),
            VMEM((channels * 16, inner), BF16),
        ],
        compiler_params=pltpu.CompilerParams(vmem_limit_bytes=(40 if inner <= 256 else 62) << 20),
        cost_estimate=SMALL,
        name="mix",
    )(info, shift, turned, own, *parcels)


def product(mixed, rights, wheres):
    total = None
    for right, where in zip(rights, wheres):
        depth = right[0].shape[1]
        column = pl.multiple_of(where * depth, depth)
        part = lax.dot_general(
            mixed[:, pl.ds(column, len(right) * depth)],
            jnp.concatenate(right, axis=1),
            (((1,), (1,)), ((), ())),
            preferred_element_type=F32,
        )
        total = part if total is None else total + part
    return total


def masked(total, info, dims, begin):
    rows, size = total.shape
    sector = info[0] * 2 + info[3]
    cube = (rows // 8, 8, size)
    a = lax.broadcasted_iota(jnp.int32, cube, 0)
    b = lax.broadcasted_iota(jnp.int32, cube, 2) + begin
    keep = (a < dims[sector]) & (b < dims[2 * info[1] - 1 - sector])
    return jnp.where(keep, total.reshape(cube), 0.0)


def others(info, v_dev, groups):
    return [lax.rem(info[2] + j, groups) * v_dev for j in range(1, groups)]


def spots_of(info, v_dev, count):
    return [info[2] * v_dev] + others(info, v_dev, count)


def give_kernel(piece, info, dims, mixed, *refs):
    rights, out = refs[:-1], refs[-1]
    v_dev, size, _ = rights[0].shape
    blocks = [[right[v] for v in range(v_dev)] for right in rights]
    total = product(mixed, blocks, spots_of(info, v_dev, len(rights)))
    cube = masked(total, info, dims, piece * size)
    half = cube.shape[0] // 2
    out[:half] = jnp.concatenate([cube[:half], cube[half:]], axis=2).astype(BF16)
    if out.shape[0] > half:
        out[half:] = jnp.zeros((1, *out.shape[1:]), BF16)


def give(piece, info, dims, mixed, rights):
    size = rights[0].shape[1]
    return pl.pallas_call(
        functools.partial(give_kernel, piece),
        out_shape=jax.ShapeDtypeStruct((mixed.shape[0] // 16 + 1 - piece, 8, 2 * size), BF16),
        in_specs=[pl.BlockSpec(memory_space=SMEM)] * 2
        + [pl.BlockSpec(memory_space=VMEM)] * (1 + len(rights)),
        out_specs=pl.BlockSpec(memory_space=VMEM),
        compiler_params=pltpu.CompilerParams(vmem_limit_bytes=24 << 20),
        cost_estimate=SOME,
        name=f"give_{piece}",
    )(info, dims, mixed, *rights)


def keep_kernel(info, dims, mixed, *refs):
    rights, out = refs[:-1], refs[-1]
    half = len(rights) // 2
    v_dev = rights[0].shape[0]
    blocks = [
        [jnp.concatenate([low[v], high[v]], axis=0) for v in range(v_dev)]
        for low, high in zip(rights[:half], rights[half:])
    ]
    total = product(mixed, blocks, spots_of(info, v_dev, half))
    out[0] = masked(total, info, dims, 0).astype(BF16)


def keep(info, dims, mixed, rights):
    rows, width = mixed.shape[0], rights[0].shape[2]
    return pl.pallas_call(
        keep_kernel,
        out_shape=jax.ShapeDtypeStruct((2, rows // 8, 8, width), BF16),
        grid_spec=pltpu.PrefetchScalarGridSpec(
            num_scalar_prefetch=2,
            grid=(1,),
            in_specs=[pl.BlockSpec(memory_space=VMEM)] * (1 + len(rights)),
            out_specs=pl.BlockSpec(
                (1, rows // 8, 8, width), lambda i, info, dims: (info[3], 0, 0, 0)
            ),
        ),
        compiler_params=pltpu.CompilerParams(vmem_limit_bytes=24 << 20),
        cost_estimate=SMALL,
        name="keep",
    )(info, dims, mixed, *rights)


def finish_kernel(info, zero, one, result, out):
    half, _, width = one.shape
    lower = lax.broadcasted_iota(jnp.int32, one.shape, 2) < width // 2

    def halves(ref):
        cube = ref[:half].astype(F32)
        turned = pltpu.roll(cube.reshape(half * 8, width), width // 2, 1)
        return cube, turned.reshape(cube.shape)

    first, first_turned = halves(zero)
    second, second_turned = halves(one)
    out[0, :half] = jnp.where(lower, first, second_turned).astype(BF16)
    out[0, half:] = jnp.where(lower, first_turned, second).astype(BF16)


def finish(info, zero, one, result):
    half, _, width = one.shape
    whole = [pl.BlockSpec(a.shape, lambda i, info: (0, 0, 0)) for a in (zero, one)]
    return pl.pallas_call(
        finish_kernel,
        out_shape=jax.ShapeDtypeStruct(result.shape, BF16),
        grid_spec=pltpu.PrefetchScalarGridSpec(
            num_scalar_prefetch=1,
            grid=(1,),
            in_specs=[*whole, pl.BlockSpec(memory_space=pl.ANY)],
            out_specs=pl.BlockSpec(
                (1, 2 * half, 8, width), lambda i, info: (1 - info[3], 0, 0, 0)
            ),
        ),
        input_output_aliases={3: 0},
        compiler_params=pltpu.CompilerParams(vmem_limit_bytes=16 << 20),
        cost_estimate=SMALL,
        name="finish",
    )(info, zero, one, result)


def after(value, *others):
    return lax.optimization_barrier((value, *others))[0]


def on_device(psi, dims, left_env, right_env, shift, mpo_coef, mpo_mask):
    sec_dev, block, states, width = psi.shape
    w_dev = left_env.shape[0]
    channels = mpo_coef.shape[1]
    groups = lax.axis_size("mpo")
    reps = lax.axis_size("rep")
    spots = ("sec", "rep")
    whole = ("sec", "mpo", "rep")
    places = lax.axis_size(spots)
    place = lax.axis_index(spots)
    group = lax.axis_index("mpo")
    parity = group % 2
    share = states // groups
    begin_given = ((group + 1 - 2 * parity) * share) // 8 * 8
    begin_kept = (group * share) // 8 * 8
    info = jnp.stack([place, places, group, parity, begin_given, begin_kept]).astype(jnp.int32)

    def swap(block, begin):
        route = []
        for low in range(begin, places - 1, 2):
            route += [(low, low + 1), (low + 1, low)]
        return lax.ppermute(block, spots, route)

    def spot(place, group):
        return (place // reps * groups + group) * reps + place % reps

    def cross(block):
        route = []
        for p in range(places):
            for g in range(0, groups, 2):
                source, target = (g + 1, g) if p % 2 == 0 else (g, g + 1)
                route.append((spot(p, source), spot(p, target)))
        return lax.ppermute(block, whole, route)

    def mirrored(block):
        return lax.ppermute(block, spots, [(i, places - 1 - i) for i in range(places)])

    def slanted(block, step):
        route = []
        for p in range(places):
            for g in range(groups):
                route.append((spot(places - 1 - p, (g + step) % groups), spot(p, g)))
        return lax.ppermute(block, whole, route)

    def beside(block):
        return lax.ppermute(block, "mpo", [(g, g ^ 1) for g in range(groups)])

    steps = range(1, groups)
    near = swap(psi, 0)
    one = cut_psi(info, psi)
    early = swap(one, 1)
    turned = turn(1, after(info, one), dims, near)
    size = width // 2
    pairs = [(j, (r, size)) for r in (0, size) for j in range(groups)]
    entries, rows = [(1 + j) % 2 for j, _ in pairs], [r for _, r in pairs]
    cuts = cut_env(after(info, turned), right_env, entries, rows)
    low, high = cuts[:groups], cuts[groups:]
    sent = pack(after(info, *cuts), mpo_mask, shift, mpo_coef, left_env, groups - 1)
    parcels = [sent[0]] + [ring(p, "mpo", j) for j, p in zip(steps, sent)]
    same = [mirrored(low[0]), mirrored(after(high[0], *sent))]
    crossed = cross(after(early, *sent))
    turned = turn(0, after(info, *sent), dims, psi, turned)
    turned = turn(2, after(info, same[0]), dims, early, turned)
    low = [slanted(after(c, turned), j) for c, j in zip(low[1:], steps)]
    high = [slanted(after(c, turned), j) for c, j in zip(high[1:], steps)]
    turned = turn(3, info, dims, crossed, turned)
    last = w_dev * block + channels * states
    shifts = jnp.concatenate([p[last, :w_dev] for p in parcels]).astype(jnp.int32)
    given, kept = mix(info, shifts, channels, turned, left_env, parcels)
    low, high = [same[0], *low], [same[1], *high]
    to_give = give(0, info, dims, given, low)
    zero = beside(to_give)
    part = give(1, after(info, to_give), dims, given, high)
    one = beside(part)
    result = keep(after(info, part), dims, kept, low + high)
    result = finish(info, zero, one, result)
    if share != 8:
        result = lax.dynamic_slice_in_dim(result, group * share - begin_kept, share, 2)
    return result


def solution(mesh):
    return jax.shard_map(
        on_device,
        mesh=mesh,
        in_specs=(
            P(("runs", "sec", "rep"), None, None, None),
            P("runs"),
            P("mpo", ("runs", "sec", "rep"), None, None),
            P("mpo", ("runs", "sec", "rep"), None, None),
            P("mpo"),
            P("mpo", None, None, None),
            P("mpo", None),
        ),
        out_specs=P(("runs", "sec", "rep"), None, "mpo", None),
        check_vma=False,
    )
```
